128 devices in a mesh: gx: 8 (over z, core), gy: 16 (over y, x).
Axes of the slice: x: 4, y: 4, z: 4, core: 2. Of those that a mesh axis runs over, the one named last changes fastest.
Arguments:
- tokens: bfloat16 [512, 8192], P('gy', 'gx'), may hold values from -7 to 7
- gain: float32 [8192], P('gx'), may hold values from 0.1 to 1.9
- gate_weight: bfloat16 [8192, 32768], P('gx', 'gy'), may hold values from -0.0625 to 0.0625
- up_weight: bfloat16 [8192, 32768], P('gx', 'gy'), may hold values from -0.0625 to 0.0625
- down_weight: bfloat16 [32768, 8192], P('gy', 'gx'), may hold values from -0.03125 to 0.03125
- query_weight: bfloat16 [8192, 8192], P('gx', 'gy'), may hold values from -0.0625 to 0.0625
- pair_weight: bfloat16 [8192, 512], P('gx', 'gy'), may hold values from -0.0625 to 0.0625
- out_weight: bfloat16 [8192, 8192], P('gy', 'gx'), may hold values from -0.0625 to 0.0625
- cache_k: bfloat16 [512, 1024, 256], P(('gx', 'gy')), may hold values from -360 to 360
- cache_v: bfloat16 [512, 1024, 256], P(('gx', 'gy')), may hold values from -6 to 6
- lengths: int32 [512], P('gx'), may hold values from 1 to 1024, as said below
Outputs:
- mixed: bfloat16 [512, 8192], P('gy', 'gx')
- new_pair: bfloat16 [512, 512], P(('gx', 'gy'))
The draws below stay inside these ranges and needn't reach their ends.
Inputs may be any that keep to these rules, and one draw needn't show every extreme that they name: `lengths`: each row has at least one cached token; the largest length equals 1024 in every draw. Cache slots at a row's length and beyond hold no history.
All inputs are finite; a program needn't handle non-finite values.
Results may differ from the reference program's by a relative error of at most 0.0093.
Values may be sent and summed in bfloat16 or wider, within the bound.
A program may use at most 128 MiB of HBM per device.

```python
import jax
import jax.numpy as jnp
from jax import lax

D = 8192
H = 32
HD = 256
FF = 32768
CACHE = 1024
ROWS = 512


def draw_tokens(key, part):
    key = jax.random.fold_in(key, 13)
    noise_key, size_key, sign_key = jax.random.split(key, 3)
    column = jnp.arange(D, dtype=jnp.float32)[None, :] / D
    magnitude = jax.random.uniform(size_key, (ROWS, 1), jnp.float32, 0.5, 1.0)
    sign = jnp.where(jax.random.bernoulli(sign_key, 0.5, (ROWS, 1)), 1.0, -1.0)
    profile = 0.5 + column
    noise = jnp.clip(jax.random.normal(noise_key, (ROWS, D), jnp.float32), -3.5, 3.5)
    noise = noise * (0.5 + column)
    return (noise + sign * magnitude * profile).astype(jnp.bfloat16)


def draw_cache_k(key, part):
    key = jax.random.fold_in(key, 11)
    base = jnp.clip(jax.random.normal(key, (ROWS, CACHE, HD), jnp.float32), -6.0, 6.0)
    return base.astype(jnp.bfloat16)


def draw_lengths(key, part):
    key = jax.random.fold_in(key, 7)
    first, second = jax.random.split(key)
    values = jax.random.randint(first, (ROWS,), 1, CACHE + 1, jnp.int32)
    chosen = jax.random.randint(second, (), 0, ROWS, jnp.int32)
    return jnp.where(jnp.arange(ROWS, dtype=jnp.int32) == chosen, CACHE, values).astype(jnp.int32)


def levels(stream_key, shape, pieces, low, top_value):
    level = 1.0
    for dim, blocks in pieces:
        steps = jax.random.uniform(jax.random.fold_in(jax.random.fold_in(stream_key, 6), dim), (blocks,), jnp.float32, low / len(pieces), top_value / len(pieces))
        level = level * jnp.repeat(jnp.exp(steps), shape[dim] // blocks).reshape((-1,) + (1,) * (len(shape) - 1 - dim))
    return level


def centred(rng, shape, scale, most, shards=(), kind=jnp.bfloat16):
    factor_of = levels(rng, shape, shards, -0.22, 0.18) if shards else 1.0
    array = jax.random.normal(rng, shape, jnp.float32) * scale * factor_of
    return jnp.minimum(jnp.maximum(array, -most), most).astype(kind)


def setup_inputs(seed: int = 0) -> dict:
    seeds = jax.random.split(jax.random.key(seed), 12)
    tokens = draw_tokens(jax.random.fold_in(seeds[11], 71), 0)
    gain = jnp.clip(1.0 + 0.18 * jax.random.normal(seeds[1], (D,), jnp.float32), 0.1, 1.9)
    gate_weight = centred(seeds[2], (D, FF), D ** -0.5, 0.0625, ((0, 8), (1, 16)))
    up_weight = centred(seeds[3], (D, FF), D ** -0.5, 0.0625, ((0, 8), (1, 16)))
    down_weight = centred(seeds[4], (FF, D), FF ** -0.5, 0.03125, ((0, 16), (1, 8)))
    query_weight = centred(seeds[5], (D, H * HD), D ** -0.5, 0.0625, ((0, 8), (1, 16)))
    pair_weight = centred(seeds[6], (D, 2 * HD), D ** -0.5, 0.0625, ((0, 8), (1, 16)))
    out_weight = centred(seeds[7], (H * HD, D), (H * HD) ** -0.5, 0.0625, ((0, 16), (1, 8)))
    cache_k = draw_cache_k(jax.random.fold_in(seeds[11], 71), 0)
    cache_v = centred(seeds[9], (ROWS, CACHE, HD), 1.0, 6.0, ((0, 128),))
    lengths = draw_lengths(jax.random.fold_in(seeds[11], 71), 0)
    return {"tokens": tokens, "gain": gain, "gate_weight": gate_weight, "up_weight": up_weight, "down_weight": down_weight, "query_weight": query_weight, "pair_weight": pair_weight, "out_weight": out_weight, "cache_k": cache_k, "cache_v": cache_v, "lengths": lengths}


EPS = 1e-05

def rotate_pairs(values, positions, first_pair, head, limit):
    rows, cols = values.shape
    pairs = values.reshape(rows, cols // 2, 2)
    index = first_pair + jnp.arange(cols // 2, dtype=jnp.int32)
    slot = (index % (head // 2)).astype(jnp.float32)
    freq = jnp.power(10000.0, -2.0 * slot / head)
    angle = positions.astype(jnp.float32)[:, None] * freq[None, :]
    cosine = jnp.cos(angle)
    sine = jnp.sin(angle)
    even = pairs[:, :, 0]
    odd = pairs[:, :, 1]
    turned = jnp.stack([even * cosine - odd * sine, even * sine + odd * cosine], axis=-1)
    keep = (2 * index < limit)[None, :, None]
    return jnp.where(keep, turned, pairs).reshape(rows, cols)

def reference(tokens, gain, gate_weight, up_weight, down_weight, query_weight, pair_weight, out_weight, cache_k, cache_v, lengths):
    values = tokens.astype(jnp.float32)
    mean = lax.optimization_barrier(jnp.mean(values, axis=1, keepdims=True))
    centered = values - mean
    spread = lax.optimization_barrier(jnp.mean(centered * centered, axis=1, keepdims=True))
    normed = (centered * lax.rsqrt(spread + EPS) * gain.astype(jnp.float32)[None, :]).astype(jnp.bfloat16)
    gate = jnp.dot(normed, gate_weight, preferred_element_type=jnp.float32)
    up = jnp.dot(normed, up_weight, preferred_element_type=jnp.float32)
    hidden = (jax.nn.silu(gate) * up).astype(jnp.bfloat16)
    query = jnp.dot(normed, query_weight, preferred_element_type=jnp.float32)
    query = rotate_pairs(query, lengths, 0, HD, H * HD).astype(jnp.bfloat16)
    pair = jnp.dot(normed, pair_weight, preferred_element_type=jnp.float32)
    new_pair = rotate_pairs(pair, lengths, 0, HD, HD).astype(jnp.bfloat16)
    scale = HD ** (-0.5)
    heads_q = query.reshape(ROWS, H, HD).astype(jnp.float32)
    new_key = new_pair[:, :HD].astype(jnp.float32)
    new_value = new_pair[:, HD:].astype(jnp.float32)
    scores = jnp.einsum('rhd,rld->rhl', heads_q, cache_k.astype(jnp.float32)) * scale
    fresh = jnp.einsum('rhd,rd->rh', heads_q, new_key) * scale
    valid = jnp.arange(CACHE, dtype=jnp.int32)[None, None, :] < lengths[:, None, None]
    top = jnp.maximum(lax.optimization_barrier(jnp.max(jnp.where(valid, scores, -1e+30), axis=2)), fresh)
    weights = jnp.where(valid, jnp.exp(scores - top[:, :, None]), 0.0)
    fresh_weight = jnp.exp(fresh - top)
    total = lax.optimization_barrier(jnp.sum(weights, axis=2)) + fresh_weight
    probs = (weights / total[:, :, None]).astype(jnp.bfloat16)
    fresh_prob = (fresh_weight / total).astype(jnp.bfloat16)
    attended = jnp.einsum('rhl,rld->rhd', probs.astype(jnp.float32), cache_v.astype(jnp.float32))
    attended = attended + fresh_prob.astype(jnp.float32)[:, :, None] * new_value[:, None, :]
    attended = attended.astype(jnp.bfloat16).reshape(ROWS, H * HD)
    total_out = jnp.dot(hidden, down_weight, preferred_element_type=jnp.float32) + jnp.dot(attended, out_weight, preferred_element_type=jnp.float32)
    mixed = (total_out + values).astype(jnp.bfloat16)
    return (mixed, new_pair)
```

```python
import jax
import jax.numpy as jnp
import numpy as np
from jax import lax
from jax.experimental import pallas as pl
from jax.experimental.pallas import tpu as pltpu
from jax.sharding import PartitionSpec as P

EPS = 1e-05
MESH = pl.DeviceIdType.MESH
F32 = jnp.float32
BF16 = jnp.bfloat16
T = 4
ROWS = 512
WIDTH = 8192
DEPTH = 1024
HID = 2048
QC = 512
PAIR = 32
HEAD = 256
SLOTS = 1024
BLK = 32
PIECE = 128
OWN = 4


def iota(shape, dim):
    return lax.broadcasted_iota(jnp.int32, shape, dim)


def dot(a, b):
    return jnp.dot(a, b, preferred_element_type=F32)


def onehot(cond):
    return jnp.where(cond, 1.0, 0.0).astype(BF16)


def kernel(
    tokens, gain, lengths, freq, gate_h, up_h, down_h, query_h, pair_w, out_h, ck_h, cv_h,
    mixed, new_pair,
    gate_w, up_w, down_w, query_w, out_w, ck, cv, pair_p,
    st, xb, part, corecv, zs, zrecv, hid,
    qpart, qcore, qsum, qz, tab, ab, arecv, qall, npair, attk, bb, brecv, att,
    total, dpart, rs,
    lsem, st_s, st_r, tok_s, tok_r, core_s, core_r, z_s, z_r, agz_s, agz_r, agc_s, agc_r,
    qc_s, qc_r, qz_s, qz_r, a_s, a_r, b_s, b_r, attz_s, attz_r, attc_s, attc_r, rs_s, rs_r,
):
    i = lax.axis_index("gx")
    j = lax.axis_index("gy")
    z, c = i // 2, i % 2
    y, x = j // 4, j % 4
    sib = (i + 1 - 2 * c, j)
    pending = []

    def zdev(k):
        return (((z + k) % 4) * 2 + c, j)

    def send(src, dst, ss, rr, dev):
        cp = pltpu.make_async_remote_copy(
            src_ref=src, dst_ref=dst, send_sem=ss, recv_sem=rr, device_id=dev, device_id_type=MESH
        )
        cp.start()
        pending.append(cp)
        return cp

    loads = {}
    for n, (name, src, dst) in enumerate(
        [
            ("gate", gate_h, gate_w), ("up", up_h, up_w), ("query", query_h, query_w),
            ("ck", ck_h, ck), ("cv", cv_h, cv), ("down", down_h, down_w), ("out", out_h, out_w),
        ]
    ):
        loads[name] = pltpu.make_async_copy(src, dst, lsem.at[n])
        loads[name].start()

    barrier = pltpu.get_barrier_semaphore()
    for k in range(1, 8):
        pl.semaphore_signal(barrier, inc=1, device_id=((i + k) % 8, j), device_id_type=MESH)
    for k in range(1, 16):
        pl.semaphore_signal(barrier, inc=1, device_id=(i, (j + k) % 16), device_id_type=MESH)

    values = tokens[...].astype(F32)
    mean_l = jnp.sum(values, axis=1, keepdims=True) * (1.0 / DEPTH)
    off = values - mean_l
    dev_l = jnp.sum(off * off, axis=1, keepdims=True)
    diag = iota((BLK, 128), 0) == iota((BLK, 128), 1)

    def to_row(col):
        return jnp.sum(jnp.where(diag, col, 0.0), axis=0, keepdims=True)

    def to_col(row):
        return jnp.sum(jnp.where(diag, row, 0.0), axis=1, keepdims=True)

    sub = iota((8, 128), 0)
    st[0] = jnp.where(sub == 0, to_row(mean_l), jnp.where(sub == 1, to_row(dev_l), 0.0))
    pl.semaphore_wait(barrier, 22)

    cps = []
    for k in range(1, 8):
        cps.append(send(st.at[0], st.at[k], st_s.at[k], st_r.at[k], ((i + k) % 8, j)))

    place = onehot(iota((PAIR, 128), 1) == iota((PAIR, 128), 0) + PAIR * (j % 4))
    pair_p[...] = dot(pair_w[...], place).astype(BF16)

    for cp in cps:
        cp.wait_recv()
    means = [st[k, 0:1, :] for k in range(8)]
    mean = means[0]
    for k in range(1, 8):
        mean = mean + means[k]
    mean = mean * 0.125
    spread = jnp.zeros_like(mean)
    for k in range(8):
        gap = means[k] - mean
        spread = spread + (st[k, 1:2, :] + DEPTH * (gap * gap))
    scale = lax.rsqrt(spread * (1.0 / WIDTH) + EPS)
    xb[0] = ((values - to_col(mean)) * to_col(scale) * gain[...]).astype(BF16)

    toks = {}
    for t in range(T):
        for dy in range(4):
            dx = (t - dy) % 4
            if dx == 0 and dy == 0:
                continue
            dst = (i, ((y + 4 - dy) % 4) * 4 + (x + 4 - dx) % 4)
            b = 4 * t + dy
            toks[b] = send(xb.at[0], xb.at[b], tok_s.at[b], tok_r.at[b], dst)

    lens = jnp.zeros((64, 128), jnp.int32)
    row64 = iota((64, 128), 0)
    for r in range(64):
        lens = jnp.where(row64 == r, lengths[r], lens)
    lens = lens[:, 0:1].astype(F32)
    angle = lens * freq[...]
    tab[0] = jnp.cos(angle)
    tab[1] = jnp.sin(angle)

    def wait_tokens(t):
        for dy in range(4):
            if 4 * t + dy in toks:
                toks[4 * t + dy].wait_recv()

    def piece_rows(t):
        return xb[4 * t : 4 * t + 4].reshape(PIECE, DEPTH)

    core = {}

    def gate_up(t):
        def body(d, carry):
            rows = piece_rows(t)
            cols = pl.ds(pl.multiple_of(d * 256, 256), 256)
            g = dot(rows, gate_w[:, cols])
            u = dot(rows, up_w[:, cols])
            part[t, d % 2, d // 2, :, 0:256] = g.astype(BF16)
            part[t, d % 2, d // 2, :, 256:512] = u.astype(BF16)
            return carry

        lax.fori_loop(0, 8, body, 0)
        core[t] = send(part.at[t, 1 - c], corecv.at[t], core_s.at[t], core_r.at[t], sib)

    zcp = {}

    def core_add(t):
        core[t].wait_recv()

        def body(k, carry):
            zs[t, k] = (part[t, c, k].astype(F32) + corecv[t, k].astype(F32)).astype(BF16)
            return carry

        lax.fori_loop(0, 4, body, 0)
        for k in (1, 3, 2):
            zcp[t, k] = send(
                zs.at[t, (z + k) % 4], zrecv.at[t, k - 1], z_s.at[t, k - 1], z_r.at[t, k - 1], zdev(k)
            )

    agz, agc = {}, {}

    def hidden_cols(k):
        owner = ((z + 4 - k) % 4) * 2 + c
        return pl.ds(pl.multiple_of(owner * 256, 256), 256)

    def finish_hidden(t):
        for k in (1, 2, 3):
            zcp[t, k].wait_recv()
        both = part[t, c, z].astype(F32) + corecv[t, z].astype(F32)
        for k in range(3):
            both = both + zrecv[t, k].astype(F32)
        g, u = both[:, 0:256], both[:, 256:512]
        h = (g / (1.0 + jnp.exp(-g)) * u).astype(BF16)
        mine = hidden_cols(0)
        hid[t, :, mine] = h
        block = hid.at[t, :, mine]
        for k in (1, 3, 2):
            agz[t, k] = send(block, block, agz_s.at[t, k - 1], agz_r.at[t, k - 1], zdev(k))
        agc[t, 0] = send(block, block, agc_s.at[t, 0], agc_r.at[t, 0], sib)

    def forward_hidden(t):
        for k in (1, 3, 2):
            agz[t, k].wait_recv()
            block = hid.at[t, :, hidden_cols(k)]
            agc[t, k] = send(block, block, agc_s.at[t, k], agc_r.at[t, k], sib)

    def down(t):
        for k in range(4):
            agc[t, k].wait_recv()

        def body(n, carry):
            cols = pl.ds(pl.multiple_of(n * 512, 512), 512)
            total[t, :, cols] = dot(hid[t], down_w[:, cols])
            return carry

        lax.fori_loop(0, 2, body, 0)

    qcp = {}

    def query_product():
        for t in range(T):
            rows = piece_rows(t)
            q = dot(rows, query_w[...])
            p = dot(rows, pair_p[...])
            for dy in range(4):
                zz = (y + dy) % 4
                xx = (x + (t - dy) % 4) % 4
                piece = slice(BLK * dy, BLK * dy + BLK)
                qpart[xx // 2, zz, xx % 2, :, 0:QC] = q[piece]
                qpart[xx // 2, zz, xx % 2, :, QC:] = p[piece]
        qcp["core"] = send(qpart.at[1 - c], qcore, qc_s.at[0], qc_r.at[0], sib)

    def query_core_add():
        qcp["core"].wait_recv()

        def body(k, carry):
            qsum[k] = qpart[c, k] + qcore[k]
            return carry

        lax.fori_loop(0, 4, body, 0)
        for k in (1, 3, 2):
            qcp[k] = send(
                qsum.at[(z + k) % 4], qz.at[k - 1], qz_s.at[k - 1], qz_r.at[k - 1], zdev(k)
            )

    def spread_matrix(h):
        out = iota((128, 64), 0)
        return onehot(
            (((out >> 2) & 1) == h) & (iota((128, 64), 1) == (out >> 3) * 4 + (out & 3))
        )

    def turn(v, cosine, sine):
        width = v.shape[1]
        even = (iota(v.shape, 1) & 1) == 0
        swap = jnp.where(even, pltpu.roll(v, width - 1, 1), pltpu.roll(v, 1, 1))
        return v * cosine + swap * jnp.where(even, -sine, sine)

    acp = {}

    def query_finish():
        for k in (1, 2, 3):
            qcp[k].wait_recv()
        full = qsum[z]
        for k in range(3):
            full = full + qz[k]
        full = full.reshape(64, QC + 128)
        cosine, sine = tab[0], tab[1]
        q0 = turn(full[:, 0:256], cosine, sine).astype(BF16)
        q1 = turn(full[:, 256:512], cosine, sine).astype(BF16)
        group = j // 4
        low, is_key = group == 0, group < 2
        pc = jnp.where(is_key, jnp.where(low, cosine[:, 0:128], cosine[:, 128:256]), 1.0)
        ps = jnp.where(is_key, jnp.where(low, sine[:, 0:128], sine[:, 128:256]), 0.0)
        pr = turn(full[:, QC:], pc, ps).astype(BF16)
        m0, m1 = spread_matrix(0), spread_matrix(1)
        ab[:, :, 0:256] = (dot(m0, q0) + dot(m1, q1)).reshape(16, 8, 256)
        ab[:, :, 256:384] = dot(m0, pr).reshape(16, 8, 128)
        for k in range(1, 16):
            to = (j + k) % 16
            acp[k] = send(ab.at[to], arecv.at[j], a_s.at[k], a_r.at[k], (i, to))
        arecv[j] = ab[j]

    bcp = {}

    def attention():
        for k in range(1, 16):
            acp[k].wait_recv()
        queries = arecv[:, :, 0:256].reshape(128, 256).astype(BF16)
        out = iota((128, 128), 0)
        inn = iota((128, 128), 1)
        order = onehot(
            ((out >> 5) == (inn & 3)) & (((out >> 1) & 15) == (inn >> 3)) & ((out & 1) == ((inn >> 2) & 1))
        )
        qall[...] = dot(order, queries).astype(BF16).reshape(OWN, 32, HEAD)
        for g in range(4):
            cols = arecv[4 * g, :, 256:384]
            for s in range(1, 4):
                cols = cols + arecv[4 * g + s, :, 256:384]
            npair[:, 128 * g : 128 * g + 128] = cols
        new_pair[...] = npair[0:OWN, :].astype(BF16)

        def body(k, carry):
            q = qall[k]
            s = lax.dot_general(
                q, ck[k], (((1,), (1,)), ((), ())), preferred_element_type=F32
            ) * (HEAD ** -0.5)
            pair = npair[pl.ds(k, 1), :]
            fresh = jnp.sum(q.astype(F32) * pair[:, 0:HEAD], axis=1, keepdims=True) * (HEAD ** -0.5)
            valid = iota((32, SLOTS), 1) < lengths[OWN * j + k]
            top = jnp.maximum(jnp.max(jnp.where(valid, s, -1e30), axis=1, keepdims=True), fresh)
            w = jnp.where(valid, jnp.exp(s - top), 0.0)
            fw = jnp.exp(fresh - top)
            tot = jnp.sum(w, axis=1, keepdims=True) + fw
            probs = (w / tot).astype(BF16)
            fp = (fw / tot).astype(BF16).astype(F32)
            attk[k] = (dot(probs, cv[k]) + fp * pair[:, HEAD:]).astype(BF16)
            return carry

        lax.fori_loop(0, OWN, body, 0)
        back = onehot(
            ((inn >> 5) == (out & 3)) & (((inn >> 1) & 15) == (out >> 3)) & ((inn & 1) == ((out >> 2) & 1))
        )
        bb[...] = dot(back, attk[...].reshape(128, HEAD)).reshape(16, 8, HEAD)
        for k in range(1, 16):
            to = (j + k) % 16
            bcp[k] = send(bb.at[to], brecv.at[j], b_s.at[k], b_r.at[k], (i, to))
        brecv[j] = bb[j]

    attz, attc = {}, {}

    def attended_spread():
        for k in range(1, 16):
            bcp[k].wait_recv()
        rows = brecv[...].reshape(128, HEAD).astype(BF16)
        inn = iota((64, 128), 1)
        for h in (0, 1):
            gather = onehot(
                (((inn >> 2) & 1) == h) & (iota((64, 128), 0) == (inn >> 3) * 4 + (inn & 3))
            )
            att[i, :, HEAD * h : HEAD * h + HEAD] = dot(gather, rows).astype(BF16)
        for k in (1, 3, 2):
            attz[k] = send(att.at[i], att.at[i], attz_s.at[k - 1], attz_r.at[k - 1], zdev(k))
        attc[0] = send(att.at[i], att.at[i], attc_s.at[0], attc_r.at[0], sib)

    def attended_forward():
        for k in (1, 3, 2):
            attz[k].wait_recv()
            block = att.at[((z + 4 - k) % 4) * 2 + c]
            attc[k] = send(block, block, attc_s.at[k], attc_r.at[k], sib)

    rcp = {}

    def out_product(t):
        blocks = []
        for dy in range(4):
            xx = (x + (t - dy) % 4) % 4
            start = pl.multiple_of((xx % 2) * BLK, BLK)
            blocks.append(att[2 * ((y + dy) % 4) + xx // 2, pl.ds(start, BLK), :])
        rows = jnp.concatenate(blocks, axis=0)
        for n in range(2):
            cols = slice(512 * n, 512 * n + 512)
            v = total[t, :, cols] + dot(rows, out_w[:, cols])
            dpart[t, :, :, cols] = v.astype(BF16).reshape(4, BLK, 512)
        for dy in range(4):
            dx = (t - dy) % 4
            if dx == 0 and dy == 0:
                continue
            b = 4 * t + dy
            dst = (i, ((y + dy) % 4) * 4 + (x + dx) % 4)
            rcp[b] = send(dpart.at[t, dy], rs.at[b], rs_s.at[b], rs_r.at[b], dst)

    loads["gate"].wait()
    loads["up"].wait()
    wait_tokens(0)
    gate_up(0)
    wait_tokens(1)
    gate_up(1)
    core_add(0)
    wait_tokens(2)
    wait_tokens(3)
    loads["query"].wait()
    query_product()
    core_add(1)
    gate_up(2)
    query_core_add()
    finish_hidden(0)
    core_add(2)
    gate_up(3)
    query_finish()
    forward_hidden(0)
    core_add(3)
    finish_hidden(1)
    loads["ck"].wait()
    loads["cv"].wait()
    attention()
    forward_hidden(1)
    loads["down"].wait()
    down(0)
    finish_hidden(2)
    attended_spread()
    forward_hidden(2)
    down(1)
    finish_hidden(3)
    attended_forward()
    down(2)
    forward_hidden(3)
    loads["out"].wait()
    for k in range(4):
        attc[k].wait_recv()
    out_product(0)
    out_product(1)
    out_product(2)
    down(3)
    out_product(3)

    result = tokens[...].astype(F32) + dpart[0, 0].astype(F32)
    for b in range(1, 16):
        rcp[b].wait_recv()
        result = result + rs[b].astype(F32)
    mixed[...] = result.astype(BF16)
    for cp in pending:
        cp.wait_send()


def local(
    tokens, gain, gate_weight, up_weight, down_weight, query_weight, pair_weight, out_weight,
    cache_k, cache_v, lengths,
):
    freq = np.power(10000.0, -2.0 * (np.arange(HEAD) // 2) / HEAD).astype(np.float32)[None, :]
    vm = pl.BlockSpec(memory_space=pltpu.VMEM)
    sm = pl.BlockSpec(memory_space=pltpu.SMEM)
    hb = pl.BlockSpec(memory_space=pl.ANY)
    dma = pltpu.SemaphoreType.DMA
    v = pltpu.VMEM
    return pl.pallas_call(
        kernel,
        out_shape=(
            jax.ShapeDtypeStruct((BLK, DEPTH), BF16),
            jax.ShapeDtypeStruct((OWN, 2 * HEAD), BF16),
        ),
        in_specs=[vm, vm, sm, vm, hb, hb, hb, hb, vm, hb, hb, hb],
        out_specs=(vm, vm),
        scratch_shapes=[
            v((DEPTH, HID), BF16), v((DEPTH, HID), BF16), v((HID, DEPTH), BF16),
            v((DEPTH, QC), BF16), v((QC, DEPTH), BF16),
            v((OWN, SLOTS, HEAD), BF16), v((OWN, SLOTS, HEAD), BF16), v((DEPTH, 128), BF16),
            v((8, 8, 128), F32), v((16, BLK, DEPTH), BF16),
            v((T, 2, 4, PIECE, 512), BF16), v((T, 4, PIECE, 512), BF16),
            v((T, 4, PIECE, 512), BF16), v((T, 3, PIECE, 512), BF16), v((T, PIECE, HID), BF16),
            v((2, 4, 2, BLK, QC + 128), F32), v((4, 2, BLK, QC + 128), F32),
            v((4, 2, BLK, QC + 128), F32), v((3, 2, BLK, QC + 128), F32),
            v((2, 64, HEAD), F32), v((16, 8, 384), F32), v((16, 8, 384), F32),
            v((OWN, 32, HEAD), BF16), v((8, 2 * HEAD), F32), v((OWN, 32, HEAD), BF16),
            v((16, 8, HEAD), F32), v((16, 8, HEAD), F32), v((8, 64, QC), BF16),
            v((T, PIECE, DEPTH), F32), v((T, 4, BLK, DEPTH), BF16), v((16, BLK, DEPTH), BF16),
            dma((7,)), dma((8,)), dma((8,)), dma((16,)), dma((16,)), dma((T,)), dma((T,)),
            dma((T, 3)), dma((T, 3)), dma((T, 3)), dma((T, 3)), dma((T, 4)), dma((T, 4)),
            dma((1,)), dma((1,)), dma((3,)), dma((3,)), dma((16,)), dma((16,)),
            dma((16,)), dma((16,)), dma((3,)), dma((3,)), dma((4,)), dma((4,)),
            dma((16,)), dma((16,)),
        ],
        compiler_params=pltpu.CompilerParams(
            collective_id=0, has_side_effects=True, vmem_limit_bytes=56 * 1024 * 1024
        ),
        cost_estimate=pl.CostEstimate(
            flops=2 * ROWS * DEPTH * 7200, bytes_accessed=20 * 1024 * 1024, transcendentals=1 << 20
        ),
        name="layer",
    )(
        tokens, gain.reshape(1, DEPTH), lengths, jnp.asarray(freq), gate_weight, up_weight,
        down_weight, query_weight, pair_weight, out_weight, cache_k, cache_v,
    )


def solution(mesh):
    in_specs = (
        P("gy", "gx"),
        P("gx"),
        P("gx", "gy"),
        P("gx", "gy"),
        P("gy", "gx"),
        P("gx", "gy"),
        P("gx", "gy"),
        P("gy", "gx"),
        P(("gx", "gy"), None, None),
        P(("gx", "gy"), None, None),
        P("gx"),
    )
    out_specs = (P("gy", "gx"), P(("gx", "gy"), None))
    return jax.shard_map(local, mesh=mesh, in_specs=in_specs, out_specs=out_specs, check_vma=False)
```

```python
import jax
import jax.numpy as jnp
import numpy as np
from jax import lax
from jax.experimental import pallas as pl
from jax.experimental.pallas import tpu as pltpu
from jax.sharding import PartitionSpec as P

EPS = 1e-05
MESH = pl.DeviceIdType.MESH
F32 = jnp.float32
BF16 = jnp.bfloat16
T = 4
ROWS = 512
WIDTH = 8192
DEPTH = 1024
HID = 2048
QC = 512
PAIR = 32
HEAD = 256
SLOTS = 1024
BLK = 32
PIECE = 128
OWN = 4


def iota(shape, dim):
    return lax.broadcasted_iota(jnp.int32, shape, dim)


def dot(a, b):
    return jnp.dot(a, b, preferred_element_type=F32)


def onehot(cond):
    return jnp.where(cond, 1.0, 0.0).astype(BF16)


def kernel(
    tokens_h, gain_h, lengths, freq_h, gate_h, up_h, down_h, query_h, pair_h, out_h, ck_h, cv_h,
    mixed, new_pair,
    tokens, gain, freq, pair_w,
    gate_w, up_w, down_w, query_w, out_w, ck, cv, pair_p,
    st, xb, part, corecv, zs, zsum, zrecv, hid,
    qpart, qcore, qsum, qfwd, qz, tab, ab, arecv, qall, npair, attk, bb, brecv, att,
    total, dpart, rs,
    lsem, st_s, st_r, tok_s, tok_r, core_s, core_r, z_s, z_r, agz_s, agz_r, agc_s, agc_r,
    qc_s, qc_r, qz_s, qz_r, a_s, a_r, b_s, b_r, attz_s, attz_r, attc_s, attc_r, rs_s, rs_r,
):
    i = lax.axis_index("gx")
    j = lax.axis_index("gy")
    z, c = i // 2, i % 2
    y, x = j // 4, j % 4
    sib = (i + 1 - 2 * c, j)
    pending = []

    def zdev(k):
        return (((z + k) % 4) * 2 + c, j)

    def send(src, dst, ss, rr, dev):
        cp = pltpu.make_async_remote_copy(
            src_ref=src, dst_ref=dst, send_sem=ss, recv_sem=rr, device_id=dev, device_id_type=MESH
        )
        cp.start()
        pending.append(cp)
        return cp

    loads = {}
    for n, (name, src, dst) in enumerate(
        [
            ("tokens", tokens_h, tokens), ("pair", pair_h, pair_w), ("gain", gain_h, gain),
            ("freq", freq_h, freq), ("gate", gate_h, gate_w), ("up", up_h, up_w), ("query", query_h, query_w),
            ("ck", ck_h, ck), ("cv", cv_h, cv), ("down", down_h, down_w), ("out", out_h, out_w),
        ]
    ):
        loads[name] = pltpu.make_async_copy(src, dst, lsem.at[n])
        loads[name].start()

    barrier = pltpu.get_barrier_semaphore()
    for k in range(1, 8):
        pl.semaphore_signal(barrier, inc=1, device_id=((i + k) % 8, j), device_id_type=MESH)
    for k in range(1, 16):
        pl.semaphore_signal(barrier, inc=1, device_id=(i, (j + k) % 16), device_id_type=MESH)

    loads["tokens"].wait()
    values = tokens[...].astype(F32)
    mean_l = jnp.sum(values, axis=1, keepdims=True) * (1.0 / DEPTH)
    off = values - mean_l
    dev_l = jnp.sum(off * off, axis=1, keepdims=True)
    diag = iota((BLK, 128), 0) == iota((BLK, 128), 1)

    def to_row(col):
        return jnp.sum(jnp.where(diag, col, 0.0), axis=0, keepdims=True)

    def to_col(row):
        return jnp.sum(jnp.where(diag, row, 0.0), axis=1, keepdims=True)

    sub = iota((8, 128), 0)
    st[0] = jnp.where(sub == 0, to_row(mean_l), jnp.where(sub == 1, to_row(dev_l), 0.0))
    pl.semaphore_wait(barrier, 22)

    cps = []
    for k in range(1, 8):
        cps.append(send(st.at[0], st.at[k], st_s.at[k], st_r.at[k], ((i + k) % 8, j)))

    place = onehot(iota((PAIR, 128), 1) == iota((PAIR, 128), 0) + PAIR * (j % 4))
    loads["pair"].wait()
    pair_p[...] = lax.dot_general(
        pair_w[...], place, (((0,), (0,)), ((), ())), preferred_element_type=F32
    ).astype(BF16)
    loads["gain"].wait()
    loads["freq"].wait()

    for cp in cps:
        cp.wait_recv()
    means = [st[k, 0:1, :] for k in range(8)]
    mean = means[0]
    for k in range(1, 8):
        mean = mean + means[k]
    mean = mean * 0.125
    spread = jnp.zeros_like(mean)
    for k in range(8):
        gap = means[k] - mean
        spread = spread + (st[k, 1:2, :] + DEPTH * (gap * gap))
    scale = lax.rsqrt(spread * (1.0 / WIDTH) + EPS)
    xb[0] = ((values - to_col(mean)) * to_col(scale) * gain[...]).astype(BF16)

    toks = {}
    for t in range(T):
        for dy in range(4):
            dx = (t - dy) % 4
            if dx == 0 and dy == 0:
                continue
            dst = (i, ((y + 4 - dy) % 4) * 4 + (x + 4 - dx) % 4)
            b = 4 * t + dy
            toks[b] = send(xb.at[0], xb.at[b], tok_s.at[b], tok_r.at[b], dst)

    lens = jnp.zeros((64, 128), jnp.int32)
    row64 = iota((64, 128), 0)
    for r in range(64):
        lens = jnp.where(row64 == r, lengths[r], lens)
    lens = lens[:, 0:1].astype(F32)
    angle = lens * freq[...]
    tab[0] = jnp.cos(angle)
    tab[1] = jnp.sin(angle)

    def wait_tokens(t):
        for dy in range(4):
            if 4 * t + dy in toks:
                toks[4 * t + dy].wait_recv()

    def piece_rows(t):
        return xb[4 * t : 4 * t + 4].reshape(PIECE, DEPTH)

    core = {}

    def gate_up(t):
        def half(cc):
            def body(k, carry):
                rows = piece_rows(t)
                cols = pl.ds(pl.multiple_of((2 * k + cc) * 256, 256), 256)
                g = dot(rows, gate_w[:, cols])
                u = dot(rows, up_w[:, cols])
                part[t, cc, k, :, 0:256] = g.astype(BF16)
                part[t, cc, k, :, 256:512] = u.astype(BF16)
                return carry

            lax.fori_loop(0, 4, body, 0)

        half(1 - c)
        core[t] = send(part.at[t, 1 - c], corecv.at[t], core_s.at[t], core_r.at[t], sib)
        half(c)

    zcp = {}

    up_dev, dn_dev = zdev(1), zdev(3)
    far, nxt, prv = (z + 2) % 4, (z + 1) % 4, (z + 3) % 4
    lo, hi = slice(0, 64), slice(64, 128)

    def core_add(t):
        core[t].wait_recv()

        def both(k):
            zs[t, k] = (part[t, c, k].astype(F32) + corecv[t, k].astype(F32)).astype(BF16)

        def go(n, src, dev):
            zcp[t, n] = send(src, zrecv.at[t, n], z_s.at[t, n], z_r.at[t, n], dev)

        both(far)
        go(0, zs.at[t, far, lo], up_dev)
        go(1, zs.at[t, far, hi], dn_dev)
        both(nxt)
        go(2, zs.at[t, nxt, hi], up_dev)
        both(prv)
        go(3, zs.at[t, prv, lo], dn_dev)

    def pass_on(t):
        for n, (to, half, dev) in enumerate(((nxt, lo, up_dev), (prv, hi, dn_dev))):
            zcp[t, n].wait_recv()
            zsum[t, n] = (zs[t, to, half].astype(F32) + zrecv[t, n].astype(F32)).astype(BF16)
            zcp[t, 4 + n] = send(
                zsum.at[t, n], zrecv.at[t, 4 + n], z_s.at[t, 4 + n], z_r.at[t, 4 + n], dev
            )

    agz, agc = {}, {}

    def hidden_cols(k):
        owner = ((z + 4 - k) % 4) * 2 + c
        return pl.ds(pl.multiple_of(owner * 256, 256), 256)

    def finish_hidden(t):
        for n in (3, 2, 4, 5):
            zcp[t, n].wait_recv()
        mine = hidden_cols(0)
        for half, n, m in ((lo, 4, 3), (hi, 2, 5)):
            v = part[t, c, z, half].astype(F32) + corecv[t, z, half].astype(F32)
            v = v + (zrecv[t, n].astype(F32) + zrecv[t, m].astype(F32))
            g, u = v[:, 0:256], v[:, 256:512]
            hid[t, half, mine] = (g / (1.0 + jnp.exp(-g)) * u).astype(BF16)
        block = hid.at[t, :, mine]
        agz[t, 0] = send(block, block, agz_s.at[t, 0], agz_r.at[t, 0], up_dev)
        agz[t, 1] = send(block, block, agz_s.at[t, 1], agz_r.at[t, 1], dn_dev)
        agc[t, 0] = send(block, block, agc_s.at[t, 0], agc_r.at[t, 0], sib)

    def forward_hidden(t):
        for n, (k, half, dev) in enumerate(((1, lo, up_dev), (3, hi, dn_dev))):
            agz[t, n].wait_recv()
            part_of = hid.at[t, half, hidden_cols(k)]
            agz[t, 2 + n] = send(part_of, part_of, agz_s.at[t, 2 + n], agz_r.at[t, 2 + n], dev)
        for n, k in ((1, 1), (2, 3)):
            block = hid.at[t, :, hidden_cols(k)]
            agc[t, n] = send(block, block, agc_s.at[t, n], agc_r.at[t, n], sib)

    def forward_far(t):
        agz[t, 2].wait_recv()
        agz[t, 3].wait_recv()
        block = hid.at[t, :, hidden_cols(2)]
        agc[t, 3] = send(block, block, agc_s.at[t, 3], agc_r.at[t, 3], sib)

    def down(t):
        for k in range(4):
            agc[t, k].wait_recv()

        def body(n, carry):
            cols = pl.ds(pl.multiple_of(n * 512, 512), 512)
            total[t, :, cols] = dot(hid[t], down_w[:, cols])
            return carry

        lax.fori_loop(0, 2, body, 0)

    qcp = {}

    def query_product():
        for t in range(T):
            rows = piece_rows(t)
            q = dot(rows, query_w[...])
            p = dot(rows, pair_p[...])
            for dy in range(4):
                zz = (y + dy) % 4
                xx = (x + (t - dy) % 4) % 4
                piece = slice(BLK * dy, BLK * dy + BLK)
                qpart[xx // 2, zz, xx % 2, :, 0:QC] = q[piece]
                qpart[xx // 2, zz, xx % 2, :, QC:] = p[piece]
        qcp["core"] = send(qpart.at[1 - c], qcore, qc_s.at[0], qc_r.at[0], sib)

    def query_core_add():
        qcp["core"].wait_recv()

        def go(n, src, dev):
            qcp[n] = send(src, qz.at[n], qz_s.at[n], qz_r.at[n], dev)

        qsum[far] = qpart[c, far] + qcore[far]
        go(0, qsum.at[far, 0], up_dev)
        go(1, qsum.at[far, 1], dn_dev)
        qsum[nxt] = qpart[c, nxt] + qcore[nxt]
        go(2, qsum.at[nxt, 1], up_dev)
        qsum[prv] = qpart[c, prv] + qcore[prv]
        go(3, qsum.at[prv, 0], dn_dev)

    def query_pass_on():
        for n, (to, half, dev) in enumerate(((nxt, 0, up_dev), (prv, 1, dn_dev))):
            qcp[n].wait_recv()
            qfwd[n] = qsum[to, half] + qz[n]
            qcp[4 + n] = send(qfwd.at[n], qz.at[4 + n], qz_s.at[4 + n], qz_r.at[4 + n], dev)

    def spread_matrix(h):
        out = iota((128, 64), 0)
        return onehot(
            (((out >> 2) & 1) == h) & (iota((128, 64), 1) == (out >> 3) * 4 + (out & 3))
        )

    def turn(v, cosine, sine):
        width = v.shape[1]
        even = (iota(v.shape, 1) & 1) == 0
        swap = jnp.where(even, pltpu.roll(v, width - 1, 1), pltpu.roll(v, 1, 1))
        return v * cosine + swap * jnp.where(even, -sine, sine)

    acp = {}

    def query_finish():
        for n in (3, 2, 4, 5):
            qcp[n].wait_recv()
        full = jnp.concatenate(
            [
                qpart[c, z, 0] + qcore[z, 0] + (qz[4] + qz[3]),
                qpart[c, z, 1] + qcore[z, 1] + (qz[2] + qz[5]),
            ],
            axis=0,
        )
        cosine, sine = tab[0], tab[1]
        q0 = turn(full[:, 0:256], cosine, sine).astype(BF16)
        q1 = turn(full[:, 256:512], cosine, sine).astype(BF16)
        group = j // 4
        low, is_key = group == 0, group < 2
        pc = jnp.where(is_key, jnp.where(low, cosine[:, 0:128], cosine[:, 128:256]), 1.0)
        ps = jnp.where(is_key, jnp.where(low, sine[:, 0:128], sine[:, 128:256]), 0.0)
        pr = turn(full[:, QC:], pc, ps).astype(BF16)
        m0, m1 = spread_matrix(0), spread_matrix(1)
        ab[:, :, 0:256] = (dot(m0, q0) + dot(m1, q1)).reshape(16, 8, 256)
        ab[:, :, 256:384] = dot(m0, pr).reshape(16, 8, 128)
        for k in range(1, 16):
            to = (j + k) % 16
            acp[k] = send(ab.at[to], arecv.at[j], a_s.at[k], a_r.at[k], (i, to))
        arecv[j] = ab[j]

    bcp = {}

    def attention():
        for k in range(1, 16):
            acp[k].wait_recv()
        queries = arecv[:, :, 0:256].reshape(128, 256).astype(BF16)
        out = iota((128, 128), 0)
        inn = iota((128, 128), 1)
        order = onehot(
            ((out >> 5) == (inn & 3)) & (((out >> 1) & 15) == (inn >> 3)) & ((out & 1) == ((inn >> 2) & 1))
        )
        qall[...] = dot(order, queries).astype(BF16).reshape(OWN, 32, HEAD)
        for g in range(4):
            cols = arecv[4 * g, :, 256:384]
            for s in range(1, 4):
                cols = cols + arecv[4 * g + s, :, 256:384]
            npair[:, 128 * g : 128 * g + 128] = cols
        new_pair[...] = npair[0:OWN, :].astype(BF16)

        def body(k, carry):
            q = qall[k]
            s = lax.dot_general(
                q, ck[k], (((1,), (1,)), ((), ())), preferred_element_type=F32
            ) * (HEAD ** -0.5)
            pair = npair[pl.ds(k, 1), :]
            fresh = jnp.sum(q.astype(F32) * pair[:, 0:HEAD], axis=1, keepdims=True) * (HEAD ** -0.5)
            valid = iota((32, SLOTS), 1) < lengths[OWN * j + k]
            top = jnp.maximum(jnp.max(jnp.where(valid, s, -1e30), axis=1, keepdims=True), fresh)
            w = jnp.where(valid, jnp.exp(s - top), 0.0)
            fw = jnp.exp(fresh - top)
            tot = jnp.sum(w, axis=1, keepdims=True) + fw
            probs = (w / tot).astype(BF16)
            fp = (fw / tot).astype(BF16).astype(F32)
            attk[k] = (dot(probs, cv[k]) + fp * pair[:, HEAD:]).astype(BF16)
            return carry

        lax.fori_loop(0, OWN, body, 0)
        back = onehot(
            ((inn >> 5) == (out & 3)) & (((inn >> 1) & 15) == (out >> 3)) & ((inn & 1) == ((out >> 2) & 1))
        )
        bb[...] = dot(back, attk[...].reshape(128, HEAD)).reshape(16, 8, HEAD)
        for k in range(1, 16):
            to = (j + k) % 16
            bcp[k] = send(bb.at[to], brecv.at[j], b_s.at[k], b_r.at[k], (i, to))
        brecv[j] = bb[j]

    attz, attc = {}, {}

    def attended_spread():
        for k in range(1, 16):
            bcp[k].wait_recv()
        rows = brecv[...].reshape(128, HEAD).astype(BF16)
        inn = iota((64, 128), 1)
        for h in (0, 1):
            gather = onehot(
                (((inn >> 2) & 1) == h) & (iota((64, 128), 0) == (inn >> 3) * 4 + (inn & 3))
            )
            att[i, :, HEAD * h : HEAD * h + HEAD] = dot(gather, rows).astype(BF16)
        block = att.at[i]
        attz[0] = send(block, block, attz_s.at[0], attz_r.at[0], up_dev)
        attz[1] = send(block, block, attz_s.at[1], attz_r.at[1], dn_dev)
        attc[0] = send(block, block, attc_s.at[0], attc_r.at[0], sib)

    def attended_forward():
        for n, (k, half, dev) in enumerate(
            ((1, slice(0, 32), up_dev), (3, slice(32, 64), dn_dev))
        ):
            attz[n].wait_recv()
            part_of = att.at[((z + 4 - k) % 4) * 2 + c, half]
            attz[2 + n] = send(part_of, part_of, attz_s.at[2 + n], attz_r.at[2 + n], dev)
        for n, k in ((1, 1), (2, 3)):
            block = att.at[((z + 4 - k) % 4) * 2 + c]
            attc[n] = send(block, block, attc_s.at[n], attc_r.at[n], sib)

    def attended_far():
        attz[2].wait_recv()
        attz[3].wait_recv()
        block = att.at[far * 2 + c]
        attc[3] = send(block, block, attc_s.at[3], attc_r.at[3], sib)

    rcp = {}

    def wait_attended():
        for k in range(4):
            attc[k].wait_recv()

    def out_product(t):
        blocks = []
        for dy in range(4):
            xx = (x + (t - dy) % 4) % 4
            start = pl.multiple_of((xx % 2) * BLK, BLK)
            blocks.append(att[2 * ((y + dy) % 4) + xx // 2, pl.ds(start, BLK), :])
        rows = jnp.concatenate(blocks, axis=0)
        for n in range(2):
            cols = slice(512 * n, 512 * n + 512)
            v = total[t, :, cols] + dot(rows, out_w[:, cols])
            dpart[t, :, :, cols] = v.astype(BF16).reshape(4, BLK, 512)
        for dy in range(4):
            dx = (t - dy) % 4
            if dx == 0 and dy == 0:
                continue
            b = 4 * t + dy
            dst = (i, ((y + dy) % 4) * 4 + (x + dx) % 4)
            rcp[b] = send(dpart.at[t, dy], rs.at[b], rs_s.at[b], rs_r.at[b], dst)

    loads["gate"].wait()
    loads["up"].wait()
    wait_tokens(0)
    gate_up(0)
    core_add(0)
    wait_tokens(1)
    gate_up(1)
    core_add(1)
    pass_on(0)
    wait_tokens(2)
    wait_tokens(3)
    loads["query"].wait()
    query_product()
    pass_on(1)
    query_core_add()
    finish_hidden(0)
    gate_up(2)
    query_pass_on()
    core_add(2)
    forward_hidden(0)
    finish_hidden(1)
    gate_up(3)
    query_finish()
    pass_on(2)
    forward_far(0)
    core_add(3)
    forward_hidden(1)
    loads["ck"].wait()
    loads["cv"].wait()
    attention()
    pass_on(3)
    finish_hidden(2)
    forward_far(1)
    loads["down"].wait()
    down(0)
    attended_spread()
    forward_hidden(2)
    finish_hidden(3)
    attended_forward()
    down(1)
    forward_far(2)
    forward_hidden(3)
    attended_far()
    down(2)
    loads["out"].wait()
    wait_attended()
    out_product(0)
    out_product(1)
    out_product(2)
    forward_far(3)
    down(3)
    out_product(3)

    result = tokens[...].astype(F32) + dpart[0, 0].astype(F32)
    for b in range(1, 16):
        rcp[b].wait_recv()
        result = result + rs[b].astype(F32)
    mixed[...] = result.astype(BF16)
    for cp in pending:
        cp.wait_send()


def local(
    tokens, gain, gate_weight, up_weight, down_weight, query_weight, pair_weight, out_weight,
    cache_k, cache_v, lengths,
):
    freq = np.power(10000.0, -2.0 * (np.arange(HEAD) // 2) / HEAD).astype(np.float32)[None, :]
    vm = pl.BlockSpec(memory_space=pltpu.VMEM)
    sm = pl.BlockSpec(memory_space=pltpu.SMEM)
    hb = pl.BlockSpec(memory_space=pl.ANY)
    dma = pltpu.SemaphoreType.DMA
    v = pltpu.VMEM
    return pl.pallas_call(
        kernel,
        out_shape=(
            jax.ShapeDtypeStruct((BLK, DEPTH), BF16),
            jax.ShapeDtypeStruct((OWN, 2 * HEAD), BF16),
        ),
        in_specs=[hb, hb, sm, hb, hb, hb, hb, hb, hb, hb, hb, hb],
        out_specs=(vm, vm),
        scratch_shapes=[
            v((BLK, DEPTH), BF16), v((1, DEPTH), F32), v((1, HEAD), F32), v((PAIR, DEPTH), BF16),
            v((DEPTH, HID), BF16), v((DEPTH, HID), BF16), v((HID, DEPTH), BF16),
            v((DEPTH, QC), BF16), v((QC, DEPTH), BF16),
            v((OWN, SLOTS, HEAD), BF16), v((OWN, SLOTS, HEAD), BF16), v((DEPTH, 128), BF16),
            v((8, 8, 128), F32), v((16, BLK, DEPTH), BF16),
            v((T, 2, 4, PIECE, 512), BF16), v((T, 4, PIECE, 512), BF16),
            v((T, 4, PIECE, 512), BF16), v((T, 2, 64, 512), BF16), v((T, 6, 64, 512), BF16),
            v((T, PIECE, HID), BF16),
            v((2, 4, 2, BLK, QC + 128), F32), v((4, 2, BLK, QC + 128), F32),
            v((4, 2, BLK, QC + 128), F32), v((2, BLK, QC + 128), F32), v((6, BLK, QC + 128), F32),
            v((2, 64, HEAD), F32), v((16, 8, 384), F32), v((16, 8, 384), F32),
            v((OWN, 32, HEAD), BF16), v((8, 2 * HEAD), F32), v((OWN, 32, HEAD), BF16),
            v((16, 8, HEAD), F32), v((16, 8, HEAD), F32), v((8, 64, QC), BF16),
            v((T, PIECE, DEPTH), F32), v((T, 4, BLK, DEPTH), BF16), v((16, BLK, DEPTH), BF16),
            dma((11,)), dma((8,)), dma((8,)), dma((16,)), dma((16,)), dma((T,)), dma((T,)),
            dma((T, 6)), dma((T, 6)), dma((T, 4)), dma((T, 4)), dma((T, 4)), dma((T, 4)),
            dma((1,)), dma((1,)), dma((6,)), dma((6,)), dma((16,)), dma((16,)),
            dma((16,)), dma((16,)), dma((4,)), dma((4,)), dma((4,)), dma((4,)),
            dma((16,)), dma((16,)),
        ],
        compiler_params=pltpu.CompilerParams(
            collective_id=0, has_side_effects=True, vmem_limit_bytes=56 * 1024 * 1024
        ),
        cost_estimate=pl.CostEstimate(
            flops=2 * ROWS * DEPTH * 7200, bytes_accessed=20 * 1024 * 1024, transcendentals=1 << 20
        ),
        name="layer",
    )(
        tokens, gain.reshape(1, DEPTH), lengths, jnp.asarray(freq), gate_weight, up_weight,
        down_weight, query_weight, pair_weight.T, out_weight, cache_k, cache_v,
    )


def solution(mesh):
    in_specs = (
        P("gy", "gx"),
        P("gx"),
        P("gx", "gy"),
        P("gx", "gy"),
        P("gy", "gx"),
        P("gx", "gy"),
        P("gx", "gy"),
        P("gy", "gx"),
        P(("gx", "gy"), None, None),
        P(("gx", "gy"), None, None),
        P("gx"),
    )
    out_specs = (P("gy", "gx"), P(("gx", "gy"), None))
    return jax.shard_map(local, mesh=mesh, in_specs=in_specs, out_specs=out_specs, check_vma=False)
```

```python
import jax
import jax.numpy as jnp
import numpy as np
from jax import lax
from jax.experimental import pallas as pl
from jax.experimental.pallas import tpu as pltpu
from jax.sharding import PartitionSpec as P

EPS = 1e-05
MESH = pl.DeviceIdType.MESH
F32 = jnp.float32
BF16 = jnp.bfloat16
T = 4
ROWS = 512
WIDTH = 8192
DEPTH = 1024
HID = 2048
QC = 512
PAIR = 32
HEAD = 256
SLOTS = 1024
BLK = 32
PIECE = 128
OWN = 4


def iota(shape, dim):
    return lax.broadcasted_iota(jnp.int32, shape, dim)


def dot(a, b):
    return jnp.dot(a, b, preferred_element_type=F32)


def onehot(cond):
    return jnp.where(cond, 1.0, 0.0).astype(BF16)


def kernel(
    tokens_h, gain_h, lengths, freq_h, gate_h, up_h, down_h, query_h, pair_h, out_h, ck_h, cv_h,
    mixed, new_pair,
    tokens, gain, freq, pair_w,
    gate_w, up_w, down_w, query_w, out_w, ck, cv, pair_p,
    st, sst, tokb, xb, part, corecv, zs, zsum, zrecv, hid,
    qpart, qcore, qsum, qfwd, qz, tab, ab, arecv, qall, npair, attk, bb, brecv, att,
    total, dpart, rs,
    lsem, st_s, st_r, ss_s, ss_r, tok_s, tok_r, core_s, core_r, z_s, z_r, agz_s, agz_r, agc_s, agc_r,
    qc_s, qc_r, qz_s, qz_r, a_s, a_r, b_s, b_r, attz_s, attz_r, attc_s, attc_r, rs_s, rs_r,
):
    i = lax.axis_index("gx")
    j = lax.axis_index("gy")
    z, c = i // 2, i % 2
    y, x = j // 4, j % 4
    sib = (i + 1 - 2 * c, j)
    pending = []

    def zdev(k):
        return (((z + k) % 4) * 2 + c, j)

    def send(src, dst, ss, rr, dev):
        cp = pltpu.make_async_remote_copy(
            src_ref=src, dst_ref=dst, send_sem=ss, recv_sem=rr, device_id=dev, device_id_type=MESH
        )
        cp.start()
        pending.append(cp)
        return cp

    loads = {}
    for n, (name, src, dst) in enumerate(
        [
            ("tokens", tokens_h, tokens), ("pair", pair_h, pair_w), ("gain", gain_h, gain),
            ("freq", freq_h, freq), ("gate", gate_h, gate_w), ("up", up_h, up_w), ("query", query_h, query_w),
            ("ck", ck_h, ck), ("cv", cv_h, cv), ("down", down_h, down_w), ("out", out_h, out_w),
        ]
    ):
        loads[name] = pltpu.make_async_copy(src, dst, lsem.at[n])
        loads[name].start()

    barrier = pltpu.get_barrier_semaphore()
    for k in range(1, 8):
        pl.semaphore_signal(barrier, inc=1, device_id=((i + k) % 8, j), device_id_type=MESH)
    for k in range(1, 16):
        pl.semaphore_signal(barrier, inc=1, device_id=(i, (j + k) % 16), device_id_type=MESH)

    peers = {}
    for t in range(T):
        for dy in range(4):
            dx = (t - dy) % 4
            if dx or dy:
                peers[4 * t + dy] = (i, ((y + 4 - dy) % 4) * 4 + (x + 4 - dx) % 4)
    toks, stats = {}, {}

    def send_tokens(t):
        for b in range(4 * t, 4 * t + 4):
            if b in peers:
                toks[b] = send(tokens, tokb.at[b], tok_s.at[b], tok_r.at[b], peers[b])

    loads["tokens"].wait()
    pl.semaphore_wait(barrier, 22)
    send_tokens(0)

    values = tokens[...].astype(F32)
    mean_l = jnp.sum(values, axis=1, keepdims=True) * (1.0 / DEPTH)
    off = values - mean_l
    dev_l = jnp.sum(off * off, axis=1, keepdims=True)
    diag = iota((BLK, 128), 0) == iota((BLK, 128), 1)

    def to_row(col):
        return jnp.sum(jnp.where(diag, col, 0.0), axis=0, keepdims=True)

    def to_col(row):
        return jnp.sum(jnp.where(diag, row, 0.0), axis=1, keepdims=True)

    sub = iota((8, 128), 0)
    st[0] = jnp.where(sub == 0, to_row(mean_l), jnp.where(sub == 1, to_row(dev_l), 0.0))
    cps = []
    for k in range(1, 8):
        cps.append(send(st.at[0], st.at[k], st_s.at[k], st_r.at[k], ((i + k) % 8, j)))
    send_tokens(1)

    place = onehot(iota((PAIR, 128), 1) == iota((PAIR, 128), 0) + PAIR * (j % 4))
    loads["pair"].wait()
    pair_p[...] = lax.dot_general(
        pair_w[...], place, (((0,), (0,)), ((), ())), preferred_element_type=F32
    ).astype(BF16)
    loads["gain"].wait()
    loads["freq"].wait()

    for cp in cps:
        cp.wait_recv()
    means = [st[k, 0:1, :] for k in range(8)]
    mean = means[0]
    for k in range(1, 8):
        mean = mean + means[k]
    mean = mean * 0.125
    spread = jnp.zeros_like(mean)
    for k in range(8):
        gap = means[k] - mean
        spread = spread + (st[k, 1:2, :] + DEPTH * (gap * gap))
    scale = lax.rsqrt(spread * (1.0 / WIDTH) + EPS)
    sst[0] = jnp.where(sub == 0, mean, jnp.where(sub == 1, scale, 0.0))
    for b in peers:
        stats[b] = send(sst.at[0], sst.at[b], ss_s.at[b], ss_r.at[b], peers[b])
    send_tokens(2)
    send_tokens(3)

    def normalize(b, rows):
        centered = rows.astype(F32) - to_col(sst[b, 0:1, :])
        xb[b] = (centered * to_col(sst[b, 1:2, :]) * gain[...]).astype(BF16)

    normalize(0, tokens[...])

    lens = jnp.zeros((64, 128), jnp.int32)
    row64 = iota((64, 128), 0)
    for r in range(64):
        lens = jnp.where(row64 == r, lengths[r], lens)
    lens = lens[:, 0:1].astype(F32)
    angle = lens * freq[...]
    tab[0] = jnp.cos(angle)
    tab[1] = jnp.sin(angle)

    def wait_tokens(t):
        for b in range(4 * t, 4 * t + 4):
            if b in toks:
                toks[b].wait_recv()
                stats[b].wait_recv()
                normalize(b, tokb[b])

    def piece_rows(t):
        return xb[4 * t : 4 * t + 4].reshape(PIECE, DEPTH)

    core = {}

    def gate_up(t, which):
        def half(cc):
            def body(k, carry):
                rows = piece_rows(t)
                cols = pl.ds(pl.multiple_of((2 * k + cc) * 256, 256), 256)
                g = dot(rows, gate_w[:, cols])
                u = dot(rows, up_w[:, cols])
                part[t, cc, k, :, 0:256] = g.astype(BF16)
                part[t, cc, k, :, 256:512] = u.astype(BF16)
                return carry

            lax.fori_loop(0, 4, body, 0)

        if which == "give":
            half(1 - c)
            core[t] = send(part.at[t, 1 - c], corecv.at[t], core_s.at[t], core_r.at[t], sib)
        else:
            half(c)

    zcp = {}

    up_dev, dn_dev = zdev(1), zdev(3)
    far, nxt, prv = (z + 2) % 4, (z + 1) % 4, (z + 3) % 4
    lo, hi = slice(0, 64), slice(64, 128)

    def core_add(t):
        core[t].wait_recv()

        def both(k):
            zs[t, k] = (part[t, c, k].astype(F32) + corecv[t, k].astype(F32)).astype(BF16)

        def go(n, src, dev):
            zcp[t, n] = send(src, zrecv.at[t, n], z_s.at[t, n], z_r.at[t, n], dev)

        both(far)
        go(0, zs.at[t, far, lo], up_dev)
        go(1, zs.at[t, far, hi], dn_dev)
        both(nxt)
        go(2, zs.at[t, nxt, hi], up_dev)
        both(prv)
        go(3, zs.at[t, prv, lo], dn_dev)

    def pass_on(t):
        for n, (to, half, dev) in enumerate(((nxt, lo, up_dev), (prv, hi, dn_dev))):
            zcp[t, n].wait_recv()
            zsum[t, n] = (zs[t, to, half].astype(F32) + zrecv[t, n].astype(F32)).astype(BF16)
            zcp[t, 4 + n] = send(
                zsum.at[t, n], zrecv.at[t, 4 + n], z_s.at[t, 4 + n], z_r.at[t, 4 + n], dev
            )

    agz, agc = {}, {}

    def hidden_cols(k):
        owner = ((z + 4 - k) % 4) * 2 + c
        return pl.ds(pl.multiple_of(owner * 256, 256), 256)

    def finish_hidden(t):
        for n in (3, 2, 4, 5):
            zcp[t, n].wait_recv()
        mine = hidden_cols(0)
        for half, n, m in ((lo, 4, 3), (hi, 2, 5)):
            v = part[t, c, z, half].astype(F32) + corecv[t, z, half].astype(F32)
            v = v + (zrecv[t, n].astype(F32) + zrecv[t, m].astype(F32))
            g, u = v[:, 0:256], v[:, 256:512]
            hid[t, half, mine] = (g / (1.0 + jnp.exp(-g)) * u).astype(BF16)
        block = hid.at[t, :, mine]
        agz[t, 0] = send(block, block, agz_s.at[t, 0], agz_r.at[t, 0], up_dev)
        agz[t, 1] = send(block, block, agz_s.at[t, 1], agz_r.at[t, 1], dn_dev)
        agc[t, 0] = send(block, block, agc_s.at[t, 0], agc_r.at[t, 0], sib)

    def forward_hidden(t):
        for n, (k, half, dev) in enumerate(((1, lo, up_dev), (3, hi, dn_dev))):
            agz[t, n].wait_recv()
            part_of = hid.at[t, half, hidden_cols(k)]
            agz[t, 2 + n] = send(part_of, part_of, agz_s.at[t, 2 + n], agz_r.at[t, 2 + n], dev)
        for n, k in ((1, 1), (2, 3)):
            block = hid.at[t, :, hidden_cols(k)]
            agc[t, n] = send(block, block, agc_s.at[t, n], agc_r.at[t, n], sib)

    def forward_far(t):
        agz[t, 2].wait_recv()
        agz[t, 3].wait_recv()
        block = hid.at[t, :, hidden_cols(2)]
        agc[t, 3] = send(block, block, agc_s.at[t, 3], agc_r.at[t, 3], sib)

    def down(t):
        for k in range(4):
            agc[t, k].wait_recv()

        def body(n, carry):
            cols = pl.ds(pl.multiple_of(n * 512, 512), 512)
            total[t, :, cols] = dot(hid[t], down_w[:, cols])
            return carry

        lax.fori_loop(0, 2, body, 0)

    qcp = {}

    def query_product(t):
        rows = piece_rows(t)
        q = dot(rows, query_w[...])
        p = dot(rows, pair_p[...])
        for dy in range(4):
            zz = (y + dy) % 4
            xx = (x + (t - dy) % 4) % 4
            piece = slice(BLK * dy, BLK * dy + BLK)
            qpart[xx // 2, zz, xx % 2, :, 0:QC] = q[piece]
            qpart[xx // 2, zz, xx % 2, :, QC:] = p[piece]

    def query_send():
        qcp["core"] = send(qpart.at[1 - c], qcore, qc_s.at[0], qc_r.at[0], sib)

    def query_core_add():
        qcp["core"].wait_recv()

        def go(n, src, dev):
            qcp[n] = send(src, qz.at[n], qz_s.at[n], qz_r.at[n], dev)

        qsum[far] = qpart[c, far] + qcore[far]
        go(0, qsum.at[far, 0], up_dev)
        go(1, qsum.at[far, 1], dn_dev)
        qsum[nxt] = qpart[c, nxt] + qcore[nxt]
        go(2, qsum.at[nxt, 1], up_dev)
        qsum[prv] = qpart[c, prv] + qcore[prv]
        go(3, qsum.at[prv, 0], dn_dev)

    def query_pass_on():
        for n, (to, half, dev) in enumerate(((nxt, 0, up_dev), (prv, 1, dn_dev))):
            qcp[n].wait_recv()
            qfwd[n] = qsum[to, half] + qz[n]
            qcp[4 + n] = send(qfwd.at[n], qz.at[4 + n], qz_s.at[4 + n], qz_r.at[4 + n], dev)

    def spread_matrix(h):
        out = iota((128, 64), 0)
        return onehot(
            (((out >> 2) & 1) == h) & (iota((128, 64), 1) == (out >> 3) * 4 + (out & 3))
        )

    def turn(v, cosine, sine):
        width = v.shape[1]
        even = (iota(v.shape, 1) & 1) == 0
        swap = jnp.where(even, pltpu.roll(v, width - 1, 1), pltpu.roll(v, 1, 1))
        return v * cosine + swap * jnp.where(even, -sine, sine)

    acp = {}

    def query_finish():
        for n in (3, 2, 4, 5):
            qcp[n].wait_recv()
        full = jnp.concatenate(
            [
                qpart[c, z, 0] + qcore[z, 0] + (qz[4] + qz[3]),
                qpart[c, z, 1] + qcore[z, 1] + (qz[2] + qz[5]),
            ],
            axis=0,
        )
        cosine, sine = tab[0], tab[1]
        q0 = turn(full[:, 0:256], cosine, sine).astype(BF16)
        q1 = turn(full[:, 256:512], cosine, sine).astype(BF16)
        group = j // 4
        low, is_key = group == 0, group < 2
        pc = jnp.where(is_key, jnp.where(low, cosine[:, 0:128], cosine[:, 128:256]), 1.0)
        ps = jnp.where(is_key, jnp.where(low, sine[:, 0:128], sine[:, 128:256]), 0.0)
        pr = turn(full[:, QC:], pc, ps).astype(BF16)
        m0, m1 = spread_matrix(0), spread_matrix(1)
        ab[:, :, 0:256] = (dot(m0, q0) + dot(m1, q1)).reshape(16, 8, 256)
        ab[:, :, 256:384] = dot(m0, pr).reshape(16, 8, 128)
        for k in range(1, 16):
            to = (j + k) % 16
            acp[k] = send(ab.at[to], arecv.at[j], a_s.at[k], a_r.at[k], (i, to))
        arecv[j] = ab[j]

    bcp = {}

    def attention():
        for k in range(1, 16):
            acp[k].wait_recv()
        queries = arecv[:, :, 0:256].reshape(128, 256).astype(BF16)
        out = iota((128, 128), 0)
        inn = iota((128, 128), 1)
        order = onehot(
            ((out >> 5) == (inn & 3)) & (((out >> 1) & 15) == (inn >> 3)) & ((out & 1) == ((inn >> 2) & 1))
        )
        qall[...] = dot(order, queries).astype(BF16).reshape(OWN, 32, HEAD)
        for g in range(4):
            cols = arecv[4 * g, :, 256:384]
            for s in range(1, 4):
                cols = cols + arecv[4 * g + s, :, 256:384]
            npair[:, 128 * g : 128 * g + 128] = cols
        new_pair[...] = npair[0:OWN, :].astype(BF16)

        def body(k, carry):
            q = qall[k]
            s = lax.dot_general(
                q, ck[k], (((1,), (1,)), ((), ())), preferred_element_type=F32
            ) * (HEAD ** -0.5)
            pair = npair[pl.ds(k, 1), :]
            fresh = jnp.sum(q.astype(F32) * pair[:, 0:HEAD], axis=1, keepdims=True) * (HEAD ** -0.5)
            valid = iota((32, SLOTS), 1) < lengths[OWN * j + k]
            top = jnp.maximum(jnp.max(jnp.where(valid, s, -1e30), axis=1, keepdims=True), fresh)
            w = jnp.where(valid, jnp.exp(s - top), 0.0)
            fw = jnp.exp(fresh - top)
            tot = jnp.sum(w, axis=1, keepdims=True) + fw
            probs = (w / tot).astype(BF16)
            fp = (fw / tot).astype(BF16).astype(F32)
            attk[k] = (dot(probs, cv[k]) + fp * pair[:, HEAD:]).astype(BF16)
            return carry

        lax.fori_loop(0, OWN, body, 0)
        back = onehot(
            ((inn >> 5) == (out & 3)) & (((inn >> 1) & 15) == (out >> 3)) & ((inn & 1) == ((out >> 2) & 1))
        )
        bb[...] = dot(back, attk[...].reshape(128, HEAD)).reshape(16, 8, HEAD)
        for k in range(1, 16):
            to = (j + k) % 16
            bcp[k] = send(bb.at[to], brecv.at[j], b_s.at[k], b_r.at[k], (i, to))
        brecv[j] = bb[j]

    attz, attc = {}, {}

    def attended_spread():
        for k in range(1, 16):
            bcp[k].wait_recv()
        rows = brecv[...].reshape(128, HEAD).astype(BF16)
        inn = iota((64, 128), 1)
        for h in (0, 1):
            gather = onehot(
                (((inn >> 2) & 1) == h) & (iota((64, 128), 0) == (inn >> 3) * 4 + (inn & 3))
            )
            att[i, :, HEAD * h : HEAD * h + HEAD] = dot(gather, rows).astype(BF16)
        block = att.at[i]
        for n, k in enumerate((1, 3, 2)):
            attz[n] = send(block, block, attz_s.at[n], attz_r.at[n], zdev(k))
        attc[3] = send(block, block, attc_s.at[3], attc_r.at[3], sib)

    def attended_forward():
        for n, k in enumerate((1, 3, 2)):
            attz[n].wait_recv()
            block = att.at[((z + 4 - k) % 4) * 2 + c]
            attc[n] = send(block, block, attc_s.at[n], attc_r.at[n], sib)

    rcp = {}

    def wait_attended():
        for k in range(4):
            attc[k].wait_recv()

    def out_product(t):
        blocks = []
        for dy in range(4):
            xx = (x + (t - dy) % 4) % 4
            start = pl.multiple_of((xx % 2) * BLK, BLK)
            blocks.append(att[2 * ((y + dy) % 4) + xx // 2, pl.ds(start, BLK), :])
        rows = jnp.concatenate(blocks, axis=0)
        for n in range(2):
            cols = slice(512 * n, 512 * n + 512)
            v = total[t, :, cols] + dot(rows, out_w[:, cols])
            dpart[t, :, :, cols] = v.astype(BF16).reshape(4, BLK, 512)
        for dy in range(4):
            dx = (t - dy) % 4
            if dx == 0 and dy == 0:
                continue
            b = 4 * t + dy
            dst = (i, ((y + dy) % 4) * 4 + (x + dx) % 4)
            rcp[b] = send(dpart.at[t, dy], rs.at[b], rs_s.at[b], rs_r.at[b], dst)

    loads["gate"].wait()
    loads["up"].wait()
    wait_tokens(0)
    gate_up(0, "give")
    gate_up(0, "keep")
    core_add(0)
    loads["query"].wait()
    query_product(0)
    wait_tokens(1)
    query_product(1)
    wait_tokens(2)
    query_product(2)
    wait_tokens(3)
    query_product(3)
    query_send()
    pass_on(0)
    gate_up(1, "give")
    query_core_add()
    gate_up(1, "keep")
    gate_up(2, "give")
    query_pass_on()
    core_add(1)
    finish_hidden(0)
    gate_up(2, "keep")
    core_add(2)
    gate_up(3, "give")
    query_finish()
    pass_on(1)
    gate_up(3, "keep")
    core_add(3)
    forward_hidden(0)
    pass_on(2)
    loads["ck"].wait()
    loads["cv"].wait()
    attention()
    finish_hidden(1)
    pass_on(3)
    forward_far(0)
    forward_hidden(1)
    finish_hidden(2)
    loads["down"].wait()
    down(0)
    attended_spread()
    finish_hidden(3)
    forward_far(1)
    forward_hidden(2)
    down(1)
    attended_forward()
    forward_far(2)
    forward_hidden(3)
    down(2)
    loads["out"].wait()
    wait_attended()
    out_product(0)
    out_product(1)
    out_product(2)
    forward_far(3)
    down(3)
    out_product(3)

    result = tokens[...].astype(F32) + dpart[0, 0].astype(F32)
    for b in range(1, 16):
        rcp[b].wait_recv()
        result = result + rs[b].astype(F32)
    mixed[...] = result.astype(BF16)
    for cp in pending:
        cp.wait_send()


def local(
    tokens, gain, gate_weight, up_weight, down_weight, query_weight, pair_weight, out_weight,
    cache_k, cache_v, lengths,
):
    freq = np.power(10000.0, -2.0 * (np.arange(HEAD) // 2) / HEAD).astype(np.float32)[None, :]
    vm = pl.BlockSpec(memory_space=pltpu.VMEM)
    sm = pl.BlockSpec(memory_space=pltpu.SMEM)
    hb = pl.BlockSpec(memory_space=pl.ANY)
    dma = pltpu.SemaphoreType.DMA
    v = pltpu.VMEM
    return pl.pallas_call(
        kernel,
        out_shape=(
            jax.ShapeDtypeStruct((BLK, DEPTH), BF16),
            jax.ShapeDtypeStruct((OWN, 2 * HEAD), BF16),
        ),
        in_specs=[hb, hb, sm, hb, hb, hb, hb, hb, hb, hb, hb, hb],
        out_specs=(vm, vm),
        scratch_shapes=[
            v((BLK, DEPTH), BF16), v((1, DEPTH), F32), v((1, HEAD), F32), v((PAIR, DEPTH), BF16),
            v((DEPTH, HID), BF16), v((DEPTH, HID), BF16), v((HID, DEPTH), BF16),
            v((DEPTH, QC), BF16), v((QC, DEPTH), BF16),
            v((OWN, SLOTS, HEAD), BF16), v((OWN, SLOTS, HEAD), BF16), v((DEPTH, 128), BF16),
            v((8, 8, 128), F32), v((16, 8, 128), F32), v((16, BLK, DEPTH), BF16),
            v((16, BLK, DEPTH), BF16),
            v((T, 2, 4, PIECE, 512), BF16), v((T, 4, PIECE, 512), BF16),
            v((T, 4, PIECE, 512), BF16), v((T, 2, 64, 512), BF16), v((T, 6, 64, 512), BF16),
            v((T, PIECE, HID), BF16),
            v((2, 4, 2, BLK, QC + 128), F32), v((4, 2, BLK, QC + 128), F32),
            v((4, 2, BLK, QC + 128), F32), v((2, BLK, QC + 128), F32), v((6, BLK, QC + 128), F32),
            v((2, 64, HEAD), F32), v((16, 8, 384), F32), v((16, 8, 384), F32),
            v((OWN, 32, HEAD), BF16), v((8, 2 * HEAD), F32), v((OWN, 32, HEAD), BF16),
            v((16, 8, HEAD), F32), v((16, 8, HEAD), F32), v((8, 64, QC), BF16),
            v((T, PIECE, DEPTH), F32), v((T, 4, BLK, DEPTH), BF16), v((16, BLK, DEPTH), BF16),
            dma((11,)), dma((8,)), dma((8,)), dma((16,)), dma((16,)), dma((16,)), dma((16,)),
            dma((T,)), dma((T,)),
            dma((T, 6)), dma((T, 6)), dma((T, 4)), dma((T, 4)), dma((T, 4)), dma((T, 4)),
            dma((1,)), dma((1,)), dma((6,)), dma((6,)), dma((16,)), dma((16,)),
            dma((16,)), dma((16,)), dma((4,)), dma((4,)), dma((4,)), dma((4,)),
            dma((16,)), dma((16,)),
        ],
        compiler_params=pltpu.CompilerParams(
            collective_id=0, has_side_effects=True, vmem_limit_bytes=56 * 1024 * 1024
        ),
        cost_estimate=pl.CostEstimate(
            flops=2 * ROWS * DEPTH * 7200, bytes_accessed=20 * 1024 * 1024, transcendentals=1 << 20
        ),
        name="layer",
    )(
        tokens, gain.reshape(1, DEPTH), lengths, jnp.asarray(freq), gate_weight, up_weight,
        down_weight, query_weight, pair_weight.T, out_weight, cache_k, cache_v,
    )


def solution(mesh):
    in_specs = (
        P("gy", "gx"),
        P("gx"),
        P("gx", "gy"),
        P("gx", "gy"),
        P("gy", "gx"),
        P("gx", "gy"),
        P("gx", "gy"),
        P("gy", "gx"),
        P(("gx", "gy"), None, None),
        P(("gx", "gy"), None, None),
        P("gx"),
    )
    out_specs = (P("gy", "gx"), P(("gx", "gy"), None))
    return jax.shard_map(local, mesh=mesh, in_specs=in_specs, out_specs=out_specs, check_vma=False)
```

```python
import jax
import jax.numpy as jnp
import numpy as np
from jax import lax
from jax.experimental import pallas as pl
from jax.experimental.pallas import tpu as pltpu
from jax.sharding import PartitionSpec as P

EPS = 1e-05
MESH = pl.DeviceIdType.MESH
F32 = jnp.float32
BF16 = jnp.bfloat16
T = 4
ROWS = 512
WIDTH = 8192
DEPTH = 1024
HID = 2048
QC = 512
PAIR = 32
HEAD = 256
SLOTS = 1024
BLK = 32
PIECE = 128
OWN = 4


def iota(shape, dim):
    return lax.broadcasted_iota(jnp.int32, shape, dim)


def dot(a, b):
    return jnp.dot(a, b, preferred_element_type=F32)


def onehot(cond):
    return jnp.where(cond, 1.0, 0.0).astype(BF16)


def kernel(
    tokens_h, gain_h, lengths, freq_h, gate_h, up_h, down_h, query_h, pair_h, out_h, ck_h, cv_h,
    mixed, new_pair,
    tokens, gain, freq, pair_w,
    gate_w, up_w, down_w, query_w, out_w, ck, cv, pair_p,
    st, sst, tokb, xb, part, corecv, zs, zsum, zrecv, hid,
    qpart, qcore, qsum, qfwd, qz, tab, ab, arecv, qall, npair, attk, bb, brecv, att,
    total, dpart, r1x, r1y, r2x, r2y, mid,
    lsem, st_s, st_r, ss_s, ss_r, tok_s, tok_r, toka_s, toka_r, core_s, core_r, z_s, z_r, agz_s, agz_r, agc_s, agc_r,
    qc_s, qc_r, qz_s, qz_r, a_s, a_r, b_s, b_r, attz_s, attz_r, attc_s, attc_r,
    r1x_s, r1x_r, r1y_s, r1y_r, r2x_s, r2x_r, r2y_s, r2y_r,
):
    i = lax.axis_index("gx")
    j = lax.axis_index("gy")
    z, c = i // 2, i % 2
    y, x = j // 4, j % 4
    sib = (i + 1 - 2 * c, j)
    pending = []

    def zdev(k):
        return (((z + k) % 4) * 2 + c, j)

    def send(src, dst, ss, rr, dev):
        cp = pltpu.make_async_remote_copy(
            src_ref=src, dst_ref=dst, send_sem=ss, recv_sem=rr, device_id=dev, device_id_type=MESH
        )
        cp.start()
        pending.append(cp)
        return cp

    loads = {}
    for n, (name, src, dst) in enumerate(
        [
            ("tokens", tokens_h, tokens), ("pair", pair_h, pair_w), ("gain", gain_h, gain),
            ("freq", freq_h, freq), ("gate", gate_h, gate_w), ("up", up_h, up_w), ("query", query_h, query_w),
            ("ck", ck_h, ck), ("cv", cv_h, cv), ("down", down_h, down_w), ("out", out_h, out_w),
        ]
    ):
        loads[name] = pltpu.make_async_copy(src, dst, lsem.at[n])
        loads[name].start()

    barrier = pltpu.get_barrier_semaphore()
    for k in range(1, 8):
        pl.semaphore_signal(barrier, inc=1, device_id=((i + k) % 8, j), device_id_type=MESH)
    for k in range(1, 16):
        pl.semaphore_signal(barrier, inc=1, device_id=(i, (j + k) % 16), device_id_type=MESH)

    peers = {}
    for t in range(T):
        for dy in range(4):
            dx = (t - dy) % 4
            if dx or dy:
                peers[4 * t + dy] = (i, ((y + 4 - dy) % 4) * 4 + (x + 4 - dx) % 4)
    toks, stats = {}, {}

    top, low = slice(0, 16), slice(16, 32)

    def place_of(dx, dy):
        return 4 * ((dx + dy) % 4) + dy

    def send_tokens():
        for d in (2, 1, 3):
            for b in (place_of(d, 0), place_of(0, d)):
                toks[b] = [send(tokens, tokb.at[b], tok_s.at[b], tok_r.at[b], peers[b])]

    def forward_tokens():
        for d in (1, 3, 2):
            toks[place_of(d, 0)][0].wait_recv()
            toks[place_of(0, d)][0].wait_recv()
        for t in range(T):
            for dy in (1, 2, 3):
                dx = (t - dy) % 4
                if dx == 0:
                    continue
                b, bx, by = place_of(dx, dy), place_of(dx, 0), place_of(0, dy)
                toks[b] = [
                    send(
                        tokb.at[bx, top], tokb.at[b, top], toka_s.at[b, 0], toka_r.at[b, 0],
                        peers[by],
                    ),
                    send(
                        tokb.at[by, low], tokb.at[b, low], toka_s.at[b, 1], toka_r.at[b, 1],
                        peers[bx],
                    ),
                ]

    loads["tokens"].wait()

    values = tokens[...].astype(F32)
    mean_l = jnp.sum(values, axis=1, keepdims=True) * (1.0 / DEPTH)
    off = values - mean_l
    dev_l = jnp.sum(off * off, axis=1, keepdims=True)
    diag = iota((BLK, 128), 0) == iota((BLK, 128), 1)

    def to_row(col):
        return jnp.sum(jnp.where(diag, col, 0.0), axis=0, keepdims=True)

    def to_col(row):
        return jnp.sum(jnp.where(diag, row, 0.0), axis=1, keepdims=True)

    sub = iota((8, 128), 0)
    st[0] = jnp.where(sub == 0, to_row(mean_l), jnp.where(sub == 1, to_row(dev_l), 0.0))
    pl.semaphore_wait(barrier, 22)
    cps = []
    for k in range(1, 8):
        cps.append(send(st.at[0], st.at[k], st_s.at[k], st_r.at[k], ((i + k) % 8, j)))
    send_tokens()

    place = onehot(iota((PAIR, 128), 1) == iota((PAIR, 128), 0) + PAIR * (j % 4))
    loads["pair"].wait()
    pair_p[...] = lax.dot_general(
        pair_w[...], place, (((0,), (0,)), ((), ())), preferred_element_type=F32
    ).astype(BF16)
    loads["gain"].wait()
    loads["freq"].wait()

    for cp in cps:
        cp.wait_recv()
    means = [st[k, 0:1, :] for k in range(8)]
    mean = means[0]
    for k in range(1, 8):
        mean = mean + means[k]
    mean = mean * 0.125
    spread = jnp.zeros_like(mean)
    for k in range(8):
        gap = means[k] - mean
        spread = spread + (st[k, 1:2, :] + DEPTH * (gap * gap))
    scale = lax.rsqrt(spread * (1.0 / WIDTH) + EPS)
    sst[0] = jnp.where(sub == 0, mean, jnp.where(sub == 1, scale, 0.0))
    for b in peers:
        stats[b] = send(sst.at[0], sst.at[b], ss_s.at[b], ss_r.at[b], peers[b])
    forward_tokens()

    def normalize(b, rows):
        centered = rows.astype(F32) - to_col(sst[b, 0:1, :])
        xb[b] = (centered * to_col(sst[b, 1:2, :]) * gain[...]).astype(BF16)

    normalize(0, tokens[...])

    lens = jnp.zeros((64, 128), jnp.int32)
    row64 = iota((64, 128), 0)
    for r in range(64):
        lens = jnp.where(row64 == r, lengths[r], lens)
    lens = lens[:, 0:1].astype(F32)
    angle = lens * freq[...]
    tab[0] = jnp.cos(angle)
    tab[1] = jnp.sin(angle)

    def wait_tokens(t):
        for b in range(4 * t, 4 * t + 4):
            if b in toks:
                for cp in toks[b][0 if len(toks[b]) == 2 else 1 :]:
                    cp.wait_recv()
                stats[b].wait_recv()
                normalize(b, tokb[b])

    def piece_rows(t):
        return xb[4 * t : 4 * t + 4].reshape(PIECE, DEPTH)

    core = {}

    def gate_up(t, which):
        def half(cc):
            def body(k, carry):
                rows = piece_rows(t)
                cols = pl.ds(pl.multiple_of((2 * k + cc) * 256, 256), 256)
                g = dot(rows, gate_w[:, cols])
                u = dot(rows, up_w[:, cols])
                part[t, cc, k, :, 0:256] = g.astype(BF16)
                part[t, cc, k, :, 256:512] = u.astype(BF16)
                return carry

            lax.fori_loop(0, 4, body, 0)

        if which == "give":
            half(1 - c)
            core[t] = send(part.at[t, 1 - c], corecv.at[t], core_s.at[t], core_r.at[t], sib)
        else:
            half(c)

    zcp = {}

    up_dev, dn_dev = zdev(1), zdev(3)
    far, nxt, prv = (z + 2) % 4, (z + 1) % 4, (z + 3) % 4
    lo, hi = slice(0, 64), slice(64, 128)

    def core_add(t):
        core[t].wait_recv()

        def both(k):
            zs[t, k] = (part[t, c, k].astype(F32) + corecv[t, k].astype(F32)).astype(BF16)

        def go(n, src, dev):
            zcp[t, n] = send(src, zrecv.at[t, n], z_s.at[t, n], z_r.at[t, n], dev)

        both(far)
        go(0, zs.at[t, far, lo], up_dev)
        go(1, zs.at[t, far, hi], dn_dev)
        both(nxt)
        go(2, zs.at[t, nxt, hi], up_dev)
        both(prv)
        go(3, zs.at[t, prv, lo], dn_dev)

    def pass_on(t):
        for n, (to, half, dev) in enumerate(((nxt, lo, up_dev), (prv, hi, dn_dev))):
            zcp[t, n].wait_recv()
            zsum[t, n] = (zs[t, to, half].astype(F32) + zrecv[t, n].astype(F32)).astype(BF16)
            zcp[t, 4 + n] = send(
                zsum.at[t, n], zrecv.at[t, 4 + n], z_s.at[t, 4 + n], z_r.at[t, 4 + n], dev
            )

    agz, agc = {}, {}

    def hidden_cols(k):
        owner = ((z + 4 - k) % 4) * 2 + c
        return pl.ds(pl.multiple_of(owner * 256, 256), 256)

    def finish_hidden(t):
        for n in (3, 2, 4, 5):
            zcp[t, n].wait_recv()
        mine = hidden_cols(0)
        for half, n, m in ((lo, 4, 3), (hi, 2, 5)):
            v = part[t, c, z, half].astype(F32) + corecv[t, z, half].astype(F32)
            v = v + (zrecv[t, n].astype(F32) + zrecv[t, m].astype(F32))
            g, u = v[:, 0:256], v[:, 256:512]
            hid[t, half, mine] = (g / (1.0 + jnp.exp(-g)) * u).astype(BF16)
        block = hid.at[t, :, mine]
        agz[t, 0] = send(block, block, agz_s.at[t, 0], agz_r.at[t, 0], up_dev)
        agz[t, 1] = send(block, block, agz_s.at[t, 1], agz_r.at[t, 1], dn_dev)
        agc[t, 0] = send(block, block, agc_s.at[t, 0], agc_r.at[t, 0], sib)

    def forward_hidden(t):
        for n, (k, half, dev) in enumerate(((1, lo, up_dev), (3, hi, dn_dev))):
            agz[t, n].wait_recv()
            part_of = hid.at[t, half, hidden_cols(k)]
            agz[t, 2 + n] = send(part_of, part_of, agz_s.at[t, 2 + n], agz_r.at[t, 2 + n], dev)
        for n, k in ((1, 1), (2, 3)):
            block = hid.at[t, :, hidden_cols(k)]
            agc[t, n] = send(block, block, agc_s.at[t, n], agc_r.at[t, n], sib)

    def forward_far(t):
        agz[t, 2].wait_recv()
        agz[t, 3].wait_recv()
        block = hid.at[t, :, hidden_cols(2)]
        agc[t, 3] = send(block, block, agc_s.at[t, 3], agc_r.at[t, 3], sib)

    def down(t):
        for k in range(4):
            agc[t, k].wait_recv()

        def body(n, carry):
            cols = pl.ds(pl.multiple_of(n * 512, 512), 512)
            total[t, :, cols] = dot(hid[t], down_w[:, cols])
            return carry

        lax.fori_loop(0, 2, body, 0)

    qcp = {}

    def query_product(t):
        rows = piece_rows(t)
        q = dot(rows, query_w[...])
        p = dot(rows, pair_p[...])
        for dy in range(4):
            zz = (y + dy) % 4
            xx = (x + (t - dy) % 4) % 4
            piece = slice(BLK * dy, BLK * dy + BLK)
            qpart[xx // 2, zz, xx % 2, :, 0:QC] = q[piece]
            qpart[xx // 2, zz, xx % 2, :, QC:] = p[piece]

    def query_send():
        qcp["core"] = send(qpart.at[1 - c], qcore, qc_s.at[0], qc_r.at[0], sib)

    def query_core_add():
        qcp["core"].wait_recv()

        def go(n, src, dev):
            qcp[n] = send(src, qz.at[n], qz_s.at[n], qz_r.at[n], dev)

        qsum[far] = qpart[c, far] + qcore[far]
        go(0, qsum.at[far, 0], up_dev)
        go(1, qsum.at[far, 1], dn_dev)
        qsum[nxt] = qpart[c, nxt] + qcore[nxt]
        go(2, qsum.at[nxt, 1], up_dev)
        qsum[prv] = qpart[c, prv] + qcore[prv]
        go(3, qsum.at[prv, 0], dn_dev)

    def query_pass_on():
        for n, (to, half, dev) in enumerate(((nxt, 0, up_dev), (prv, 1, dn_dev))):
            qcp[n].wait_recv()
            qfwd[n] = qsum[to, half] + qz[n]
            qcp[4 + n] = send(qfwd.at[n], qz.at[4 + n], qz_s.at[4 + n], qz_r.at[4 + n], dev)

    def spread_matrix(h):
        out = iota((128, 64), 0)
        return onehot(
            (((out >> 2) & 1) == h) & (iota((128, 64), 1) == (out >> 3) * 4 + (out & 3))
        )

    def turn(v, cosine, sine):
        width = v.shape[1]
        even = (iota(v.shape, 1) & 1) == 0
        swap = jnp.where(even, pltpu.roll(v, width - 1, 1), pltpu.roll(v, 1, 1))
        return v * cosine + swap * jnp.where(even, -sine, sine)

    acp = {}

    def query_finish():
        for n in (3, 2, 4, 5):
            qcp[n].wait_recv()
        full = jnp.concatenate(
            [
                qpart[c, z, 0] + qcore[z, 0] + (qz[4] + qz[3]),
                qpart[c, z, 1] + qcore[z, 1] + (qz[2] + qz[5]),
            ],
            axis=0,
        )
        cosine, sine = tab[0], tab[1]
        q0 = turn(full[:, 0:256], cosine, sine).astype(BF16)
        q1 = turn(full[:, 256:512], cosine, sine).astype(BF16)
        group = j // 4
        low, is_key = group == 0, group < 2
        pc = jnp.where(is_key, jnp.where(low, cosine[:, 0:128], cosine[:, 128:256]), 1.0)
        ps = jnp.where(is_key, jnp.where(low, sine[:, 0:128], sine[:, 128:256]), 0.0)
        pr = turn(full[:, QC:], pc, ps).astype(BF16)
        m0, m1 = spread_matrix(0), spread_matrix(1)
        ab[:, :, 0:256] = (dot(m0, q0) + dot(m1, q1)).reshape(16, 8, 256)
        ab[:, :, 256:384] = dot(m0, pr).reshape(16, 8, 128)
        for k in range(1, 16):
            to = (j + k) % 16
            acp[k] = send(ab.at[to], arecv.at[j], a_s.at[k], a_r.at[k], (i, to))
        arecv[j] = ab[j]

    bcp = {}

    def attention():
        for k in range(1, 16):
            acp[k].wait_recv()
        queries = arecv[:, :, 0:256].reshape(128, 256).astype(BF16)
        out = iota((128, 128), 0)
        inn = iota((128, 128), 1)
        order = onehot(
            ((out >> 5) == (inn & 3)) & (((out >> 1) & 15) == (inn >> 3)) & ((out & 1) == ((inn >> 2) & 1))
        )
        qall[...] = dot(order, queries).astype(BF16).reshape(OWN, 32, HEAD)
        for g in range(4):
            cols = arecv[4 * g, :, 256:384]
            for s in range(1, 4):
                cols = cols + arecv[4 * g + s, :, 256:384]
            npair[:, 128 * g : 128 * g + 128] = cols
        new_pair[...] = npair[0:OWN, :].astype(BF16)

        def body(k, carry):
            q = qall[k]
            s = lax.dot_general(
                q, ck[k], (((1,), (1,)), ((), ())), preferred_element_type=F32
            ) * (HEAD ** -0.5)
            pair = npair[pl.ds(k, 1), :]
            fresh = jnp.sum(q.astype(F32) * pair[:, 0:HEAD], axis=1, keepdims=True) * (HEAD ** -0.5)
            valid = iota((32, SLOTS), 1) < lengths[OWN * j + k]
            top = jnp.maximum(jnp.max(jnp.where(valid, s, -1e30), axis=1, keepdims=True), fresh)
            w = jnp.where(valid, jnp.exp(s - top), 0.0)
            fw = jnp.exp(fresh - top)
            tot = jnp.sum(w, axis=1, keepdims=True) + fw
            probs = (w / tot).astype(BF16)
            fp = (fw / tot).astype(BF16).astype(F32)
            attk[k] = (dot(probs, cv[k]) + fp * pair[:, HEAD:]).astype(BF16)
            return carry

        lax.fori_loop(0, OWN, body, 0)
        back = onehot(
            ((inn >> 5) == (out & 3)) & (((inn >> 1) & 15) == (out >> 3)) & ((inn & 1) == ((out >> 2) & 1))
        )
        bb[...] = dot(back, attk[...].reshape(128, HEAD)).reshape(16, 8, HEAD)
        for k in range(1, 16):
            to = (j + k) % 16
            bcp[k] = send(bb.at[to], brecv.at[j], b_s.at[k], b_r.at[k], (i, to))
        brecv[j] = bb[j]

    attz, attc = {}, {}

    def attended_spread():
        for k in range(1, 16):
            bcp[k].wait_recv()
        rows = brecv[...].reshape(128, HEAD).astype(BF16)
        inn = iota((64, 128), 1)
        for h in (0, 1):
            gather = onehot(
                (((inn >> 2) & 1) == h) & (iota((64, 128), 0) == (inn >> 3) * 4 + (inn & 3))
            )
            att[i, :, HEAD * h : HEAD * h + HEAD] = dot(gather, rows).astype(BF16)
        block = att.at[i]
        for n, k in enumerate((1, 3, 2)):
            attz[n] = send(block, block, attz_s.at[n], attz_r.at[n], zdev(k))
        attc[3] = send(block, block, attc_s.at[3], attc_r.at[3], sib)

    def attended_forward():
        for n, k in enumerate((1, 3, 2)):
            attz[n].wait_recv()
            block = att.at[((z + 4 - k) % 4) * 2 + c]
            attc[n] = send(block, block, attc_s.at[n], attc_r.at[n], sib)

    r1 = {}

    def along_x(d):
        return (i, y * 4 + (x + d) % 4)

    def along_y(d):
        return (i, ((y + d) % 4) * 4 + x)

    def wait_attended():
        for k in range(4):
            attc[k].wait_recv()

    def out_product(t):
        blocks = []
        for dy in range(4):
            xx = (x + (t - dy) % 4) % 4
            start = pl.multiple_of((xx % 2) * BLK, BLK)
            blocks.append(att[2 * ((y + dy) % 4) + xx // 2, pl.ds(start, BLK), :])
        rows = jnp.concatenate(blocks, axis=0)
        for n in range(2):
            cols = slice(512 * n, 512 * n + 512)
            v = total[t, :, cols] + dot(rows, out_w[:, cols])
            dpart[t, :, :, cols] = v.astype(BF16).reshape(4, BLK, 512)
        for dy in range(4):
            dx = (t - dy) % 4
            if dx:
                r1[0, dx, dy] = send(
                    dpart.at[t, dy, top], r1x.at[dx, dy], r1x_s.at[dx, dy], r1x_r.at[dx, dy], along_x(dx)
                )
            if dy:
                r1[1, dy, dx] = send(
                    dpart.at[t, dy, low], r1y.at[dy, dx], r1y_s.at[dy, dx], r1y_r.at[dy, dx], along_y(dy)
                )

    def gathered(axis, d):
        rows, recv = (top, r1x) if axis == 0 else (low, r1y)
        v = dpart[d, d if axis == 0 else 0, rows].astype(F32)
        for e in (1, 2, 3):
            r1[axis, e, d].wait_recv()
            v = v + recv[e, d].astype(F32)
        return v

    loads["gate"].wait()
    loads["up"].wait()
    wait_tokens(0)
    gate_up(0, "give")
    gate_up(0, "keep")
    core_add(0)
    loads["query"].wait()
    query_product(0)
    wait_tokens(1)
    query_product(1)
    wait_tokens(2)
    query_product(2)
    wait_tokens(3)
    query_product(3)
    query_send()
    pass_on(0)
    gate_up(1, "give")
    query_core_add()
    gate_up(1, "keep")
    gate_up(2, "give")
    query_pass_on()
    core_add(1)
    finish_hidden(0)
    gate_up(2, "keep")
    core_add(2)
    gate_up(3, "give")
    query_finish()
    pass_on(1)
    gate_up(3, "keep")
    core_add(3)
    forward_hidden(0)
    pass_on(2)
    loads["ck"].wait()
    loads["cv"].wait()
    attention()
    finish_hidden(1)
    pass_on(3)
    forward_far(0)
    forward_hidden(1)
    finish_hidden(2)
    loads["down"].wait()
    down(0)
    attended_spread()
    finish_hidden(3)
    forward_far(1)
    forward_hidden(2)
    down(1)
    attended_forward()
    forward_far(2)
    forward_hidden(3)
    down(2)
    loads["out"].wait()
    wait_attended()
    out_product(0)
    out_product(1)
    out_product(2)
    forward_far(3)
    down(3)
    out_product(3)

    r2 = {}
    for d in (2, 1, 3):
        mid[0, d] = gathered(0, d).astype(BF16)
        r2[0, d] = send(mid.at[0, d], r2x.at[d], r2x_s.at[d], r2x_r.at[d], along_y(d))
        mid[1, d] = gathered(1, d).astype(BF16)
        r2[1, d] = send(mid.at[1, d], r2y.at[d], r2y_s.at[d], r2y_r.at[d], along_x(d))
    for axis, (rows, recv) in enumerate(((top, r2x), (low, r2y))):
        result = tokens[rows, :].astype(F32) + gathered(axis, 0)
        for d in (1, 3, 2):
            r2[axis, d].wait_recv()
            result = result + recv[d].astype(F32)
        mixed[rows, :] = result.astype(BF16)
    for cp in pending:
        cp.wait_send()


def local(
    tokens, gain, gate_weight, up_weight, down_weight, query_weight, pair_weight, out_weight,
    cache_k, cache_v, lengths,
):
    freq = np.power(10000.0, -2.0 * (np.arange(HEAD) // 2) / HEAD).astype(np.float32)[None, :]
    vm = pl.BlockSpec(memory_space=pltpu.VMEM)
    sm = pl.BlockSpec(memory_space=pltpu.SMEM)
    hb = pl.BlockSpec(memory_space=pl.ANY)
    dma = pltpu.SemaphoreType.DMA
    v = pltpu.VMEM
    return pl.pallas_call(
        kernel,
        out_shape=(
            jax.ShapeDtypeStruct((BLK, DEPTH), BF16),
            jax.ShapeDtypeStruct((OWN, 2 * HEAD), BF16),
        ),
        in_specs=[hb, hb, sm, hb, hb, hb, hb, hb, hb, hb, hb, hb],
        out_specs=(vm, vm),
        scratch_shapes=[
            v((BLK, DEPTH), BF16), v((1, DEPTH), F32), v((1, HEAD), F32), v((PAIR, DEPTH), BF16),
            v((DEPTH, HID), BF16), v((DEPTH, HID), BF16), v((HID, DEPTH), BF16),
            v((DEPTH, QC), BF16), v((QC, DEPTH), BF16),
            v((OWN, SLOTS, HEAD), BF16), v((OWN, SLOTS, HEAD), BF16), v((DEPTH, 128), BF16),
            v((8, 8, 128), F32), v((16, 8, 128), F32), v((16, BLK, DEPTH), BF16),
            v((16, BLK, DEPTH), BF16),
            v((T, 2, 4, PIECE, 512), BF16), v((T, 4, PIECE, 512), BF16),
            v((T, 4, PIECE, 512), BF16), v((T, 2, 64, 512), BF16), v((T, 6, 64, 512), BF16),
            v((T, PIECE, HID), BF16),
            v((2, 4, 2, BLK, QC + 128), F32), v((4, 2, BLK, QC + 128), F32),
            v((4, 2, BLK, QC + 128), F32), v((2, BLK, QC + 128), F32), v((6, BLK, QC + 128), F32),
            v((2, 64, HEAD), F32), v((16, 8, 384), F32), v((16, 8, 384), F32),
            v((OWN, 32, HEAD), BF16), v((8, 2 * HEAD), F32), v((OWN, 32, HEAD), BF16),
            v((16, 8, HEAD), F32), v((16, 8, HEAD), F32), v((8, 64, QC), BF16),
            v((T, PIECE, DEPTH), F32), v((T, 4, BLK, DEPTH), BF16), v((4, 4, 16, DEPTH), BF16),
            v((4, 4, 16, DEPTH), BF16), v((4, 16, DEPTH), BF16), v((4, 16, DEPTH), BF16),
            v((2, 4, 16, DEPTH), BF16),
            dma((11,)), dma((8,)), dma((8,)), dma((16,)), dma((16,)), dma((16,)), dma((16,)),
            dma((16, 2)), dma((16, 2)), dma((T,)), dma((T,)),
            dma((T, 6)), dma((T, 6)), dma((T, 4)), dma((T, 4)), dma((T, 4)), dma((T, 4)),
            dma((1,)), dma((1,)), dma((6,)), dma((6,)), dma((16,)), dma((16,)),
            dma((16,)), dma((16,)), dma((4,)), dma((4,)), dma((4,)), dma((4,)),
            dma((4, 4)), dma((4, 4)), dma((4, 4)), dma((4, 4)), dma((4,)), dma((4,)), dma((4,)), dma((4,)),
        ],
        compiler_params=pltpu.CompilerParams(
            collective_id=0, has_side_effects=True, vmem_limit_bytes=56 * 1024 * 1024
        ),
        cost_estimate=pl.CostEstimate(
            flops=2 * ROWS * DEPTH * 7200, bytes_accessed=20 * 1024 * 1024, transcendentals=1 << 20
        ),
        name="layer",
    )(
        tokens, gain.reshape(1, DEPTH), lengths, jnp.asarray(freq), gate_weight, up_weight,
        down_weight, query_weight, pair_weight.T, out_weight, cache_k, cache_v,
    )


def solution(mesh):
    in_specs = (
        P("gy", "gx"),
        P("gx"),
        P("gx", "gy"),
        P("gx", "gy"),
        P("gy", "gx"),
        P("gx", "gy"),
        P("gx", "gy"),
        P("gy", "gx"),
        P(("gx", "gy"), None, None),
        P(("gx", "gy"), None, None),
        P("gx"),
    )
    out_specs = (P("gy", "gx"), P(("gx", "gy"), None))
    return jax.shard_map(local, mesh=mesh, in_specs=in_specs, out_specs=out_specs, check_vma=False)
```

```python
import jax
import jax.numpy as jnp
import numpy as np
from jax import lax
from jax.experimental import pallas as pl
from jax.experimental.pallas import tpu as pltpu
from jax.sharding import PartitionSpec as P

EPS = 1e-05
MESH = pl.DeviceIdType.MESH
F32 = jnp.float32
BF16 = jnp.bfloat16
T = 4
ROWS = 512
WIDTH = 8192
DEPTH = 1024
HID = 2048
QC = 512
PAIR = 32
HEAD = 256
SLOTS = 1024
BLK = 32
PIECE = 128
OWN = 4


def iota(shape, dim):
    return lax.broadcasted_iota(jnp.int32, shape, dim)


def dot(a, b):
    return jnp.dot(a, b, preferred_element_type=F32)


def onehot(cond):
    return jnp.where(cond, 1.0, 0.0).astype(BF16)


def kernel(
    tokens_h, gain_h, lengths, freq_h, gate_h, up_h, down_h, query_h, pair_h, out_h, ck_h, cv_h,
    mixed, new_pair,
    tokens, gain, freq, pair_w,
    gate_w, up_w, down_w, query_w, out_w, ck, cv, pair_p,
    st, sst, tokb, xb, part, corecv, zs, zsum, zrecv, hid,
    qpart, qcore, qsum, qfwd, qz, tab, ab, arecv, qall, npair, attk, bb, brecv, att,
    total, dpart, r1x, r1y, r2x, r2y, mid,
    lsem, st_s, st_r, ss_s, ss_r, tok_s, tok_r, toka_s, toka_r, core_s, core_r, z_s, z_r, agz_s, agz_r, agc_s, agc_r,
    qc_s, qc_r, qz_s, qz_r, a_s, a_r, b_s, b_r, attz_s, attz_r, attc_s, attc_r,
    r1x_s, r1x_r, r1y_s, r1y_r, r2x_s, r2x_r, r2y_s, r2y_r,
):
    i = lax.axis_index("gx")
    j = lax.axis_index("gy")
    z, c = i // 2, i % 2
    y, x = j // 4, j % 4
    sib = (i + 1 - 2 * c, j)
    pending = []

    def zdev(k):
        return (((z + k) % 4) * 2 + c, j)

    def send(src, dst, ss, rr, dev):
        cp = pltpu.make_async_remote_copy(
            src_ref=src, dst_ref=dst, send_sem=ss, recv_sem=rr, device_id=dev, device_id_type=MESH
        )
        cp.start()
        pending.append(cp)
        return cp

    loads = {}
    for n, (name, src, dst) in enumerate(
        [
            ("tokens", tokens_h, tokens), ("pair", pair_h, pair_w), ("gain", gain_h, gain),
            ("freq", freq_h, freq), ("gate", gate_h, gate_w), ("up", up_h, up_w), ("query", query_h, query_w),
            ("ck", ck_h, ck), ("cv", cv_h, cv), ("down", down_h, down_w), ("out", out_h, out_w),
        ]
    ):
        loads[name] = pltpu.make_async_copy(src, dst, lsem.at[n])
        loads[name].start()

    barrier = pltpu.get_barrier_semaphore()
    for k in range(1, 8):
        pl.semaphore_signal(barrier, inc=1, device_id=((i + k) % 8, j), device_id_type=MESH)
    for k in range(1, 16):
        pl.semaphore_signal(barrier, inc=1, device_id=(i, (j + k) % 16), device_id_type=MESH)

    peers = {}
    for t in range(T):
        for dy in range(4):
            dx = (t - dy) % 4
            if dx or dy:
                peers[4 * t + dy] = (i, ((y + 4 - dy) % 4) * 4 + (x + 4 - dx) % 4)
    toks, stats = {}, {}

    top, low = slice(0, 16), slice(16, 32)

    def place_of(dx, dy):
        return 4 * ((dx + dy) % 4) + dy

    def send_tokens():
        for d in (2, 1, 3):
            for b in (place_of(d, 0), place_of(0, d)):
                toks[b] = [send(tokens, tokb.at[b], tok_s.at[b], tok_r.at[b], peers[b])]

    def forward_tokens():
        for d in (1, 3, 2):
            toks[place_of(d, 0)][0].wait_recv()
            toks[place_of(0, d)][0].wait_recv()
        for t in range(T):
            for dy in (1, 2, 3):
                dx = (t - dy) % 4
                if dx == 0:
                    continue
                b, bx, by = place_of(dx, dy), place_of(dx, 0), place_of(0, dy)
                toks[b] = [
                    send(
                        tokb.at[bx, top], tokb.at[b, top], toka_s.at[b, 0], toka_r.at[b, 0],
                        peers[by],
                    ),
                    send(
                        tokb.at[by, low], tokb.at[b, low], toka_s.at[b, 1], toka_r.at[b, 1],
                        peers[bx],
                    ),
                ]

    loads["tokens"].wait()

    values = tokens[...].astype(F32)
    mean_l = jnp.sum(values, axis=1, keepdims=True) * (1.0 / DEPTH)
    off = values - mean_l
    dev_l = jnp.sum(off * off, axis=1, keepdims=True)
    diag = iota((BLK, 128), 0) == iota((BLK, 128), 1)

    def to_row(col):
        return jnp.sum(jnp.where(diag, col, 0.0), axis=0, keepdims=True)

    def to_col(row):
        return jnp.sum(jnp.where(diag, row, 0.0), axis=1, keepdims=True)

    sub = iota((8, 128), 0)
    st[0] = jnp.where(sub == 0, to_row(mean_l), jnp.where(sub == 1, to_row(dev_l), 0.0))
    pl.semaphore_wait(barrier, 22)
    cps = []
    for k in range(1, 8):
        cps.append(send(st.at[0], st.at[k], st_s.at[k], st_r.at[k], ((i + k) % 8, j)))
    send_tokens()

    place = onehot(iota((PAIR, 128), 1) == iota((PAIR, 128), 0) + PAIR * (j % 4))
    loads["pair"].wait()
    pair_p[...] = lax.dot_general(
        pair_w[...], place, (((0,), (0,)), ((), ())), preferred_element_type=F32
    ).astype(BF16)
    loads["gain"].wait()
    loads["freq"].wait()

    for cp in cps:
        cp.wait_recv()
    means = [st[k, 0:1, :] for k in range(8)]
    mean = means[0]
    for k in range(1, 8):
        mean = mean + means[k]
    mean = mean * 0.125
    spread = jnp.zeros_like(mean)
    for k in range(8):
        gap = means[k] - mean
        spread = spread + (st[k, 1:2, :] + DEPTH * (gap * gap))
    scale = lax.rsqrt(spread * (1.0 / WIDTH) + EPS)
    sst[0] = jnp.where(sub == 0, mean, jnp.where(sub == 1, scale, 0.0))
    for b in peers:
        stats[b] = send(sst.at[0], sst.at[b], ss_s.at[b], ss_r.at[b], peers[b])
    forward_tokens()

    def normalize(b, rows):
        centered = rows.astype(F32) - to_col(sst[b, 0:1, :])
        xb[b] = (centered * to_col(sst[b, 1:2, :]) * gain[...]).astype(BF16)

    normalize(0, tokens[...])

    lens = jnp.zeros((64, 128), jnp.int32)
    row64 = iota((64, 128), 0)
    for r in range(64):
        lens = jnp.where(row64 == r, lengths[r], lens)
    lens = lens[:, 0:1].astype(F32)
    angle = lens * freq[...]
    tab[0] = jnp.cos(angle)
    tab[1] = jnp.sin(angle)

    def wait_tokens(t):
        for b in range(4 * t, 4 * t + 4):
            if b in toks:
                for cp in toks[b][0 if len(toks[b]) == 2 else 1 :]:
                    cp.wait_recv()
                stats[b].wait_recv()
                normalize(b, tokb[b])

    def piece_rows(t):
        return xb[4 * t : 4 * t + 4].reshape(PIECE, DEPTH)

    core = {}

    def gate_up(t, which):
        def half(cc):
            def body(k, carry):
                rows = piece_rows(t)
                cols = pl.ds(pl.multiple_of((2 * k + cc) * 256, 256), 256)
                g = dot(rows, gate_w[:, cols])
                u = dot(rows, up_w[:, cols])
                part[t, cc, k, :, 0:256] = g.astype(BF16)
                part[t, cc, k, :, 256:512] = u.astype(BF16)
                return carry

            lax.fori_loop(0, 4, body, 0)

        if which == "give":
            half(1 - c)
            core[t] = send(part.at[t, 1 - c], corecv.at[t], core_s.at[t], core_r.at[t], sib)
        else:
            half(c)

    zcp = {}

    up_dev, dn_dev = zdev(1), zdev(3)
    far, nxt, prv = (z + 2) % 4, (z + 1) % 4, (z + 3) % 4
    lo, hi = slice(0, 64), slice(64, 128)

    def core_add(t):
        core[t].wait_recv()

        def both(k):
            zs[t, k] = (part[t, c, k].astype(F32) + corecv[t, k].astype(F32)).astype(BF16)

        def go(n, src, dev):
            zcp[t, n] = send(src, zrecv.at[t, n], z_s.at[t, n], z_r.at[t, n], dev)

        both(far)
        go(0, zs.at[t, far, lo], up_dev)
        go(1, zs.at[t, far, hi], dn_dev)
        both(nxt)
        go(2, zs.at[t, nxt, hi], up_dev)
        both(prv)
        go(3, zs.at[t, prv, lo], dn_dev)

    def pass_on(t):
        for n, (to, half, dev) in enumerate(((nxt, lo, up_dev), (prv, hi, dn_dev))):
            zcp[t, n].wait_recv()
            zsum[t, n] = (zs[t, to, half].astype(F32) + zrecv[t, n].astype(F32)).astype(BF16)
            zcp[t, 4 + n] = send(
                zsum.at[t, n], zrecv.at[t, 4 + n], z_s.at[t, 4 + n], z_r.at[t, 4 + n], dev
            )

    agz, agc = {}, {}

    def hidden_cols(k):
        owner = ((z + 4 - k) % 4) * 2 + c
        return pl.ds(pl.multiple_of(owner * 256, 256), 256)

    def finish_hidden(t):
        for n in (3, 2, 4, 5):
            zcp[t, n].wait_recv()
        mine = hidden_cols(0)
        for half, n, m in ((lo, 4, 3), (hi, 2, 5)):
            v = part[t, c, z, half].astype(F32) + corecv[t, z, half].astype(F32)
            v = v + (zrecv[t, n].astype(F32) + zrecv[t, m].astype(F32))
            g, u = v[:, 0:256], v[:, 256:512]
            hid[t, half, mine] = (g / (1.0 + jnp.exp(-g)) * u).astype(BF16)
        block = hid.at[t, :, mine]
        agz[t, 0] = send(block, block, agz_s.at[t, 0], agz_r.at[t, 0], up_dev)
        agz[t, 1] = send(block, block, agz_s.at[t, 1], agz_r.at[t, 1], dn_dev)
        agc[t, 0] = send(block, block, agc_s.at[t, 0], agc_r.at[t, 0], sib)

    def forward_hidden(t):
        for n, (k, half, dev) in enumerate(((1, lo, up_dev), (3, hi, dn_dev))):
            agz[t, n].wait_recv()
            part_of = hid.at[t, half, hidden_cols(k)]
            agz[t, 2 + n] = send(part_of, part_of, agz_s.at[t, 2 + n], agz_r.at[t, 2 + n], dev)
        for n, k in ((1, 1), (2, 3)):
            block = hid.at[t, :, hidden_cols(k)]
            agc[t, n] = send(block, block, agc_s.at[t, n], agc_r.at[t, n], sib)

    def forward_far(t):
        agz[t, 2].wait_recv()
        agz[t, 3].wait_recv()
        block = hid.at[t, :, hidden_cols(2)]
        agc[t, 3] = send(block, block, agc_s.at[t, 3], agc_r.at[t, 3], sib)

    def down(t):
        for k in range(4):
            agc[t, k].wait_recv()

        def body(n, carry):
            cols = pl.ds(pl.multiple_of(n * 512, 512), 512)
            total[t, :, cols] = dot(hid[t], down_w[:, cols])
            return carry

        lax.fori_loop(0, 2, body, 0)

    qcp = {}

    def query_product(t):
        rows = piece_rows(t)
        q = dot(rows, query_w[...])
        p = dot(rows, pair_p[...])
        for dy in range(4):
            zz = (y + dy) % 4
            xx = (x + (t - dy) % 4) % 4
            piece = slice(BLK * dy, BLK * dy + BLK)
            qpart[xx // 2, zz, xx % 2, :, 0:QC] = q[piece]
            qpart[xx // 2, zz, xx % 2, :, QC:] = p[piece]

    def query_send():
        qcp["core"] = send(qpart.at[1 - c], qcore, qc_s.at[0], qc_r.at[0], sib)

    def query_core_add():
        qcp["core"].wait_recv()

        def go(n, src, dev):
            qcp[n] = send(src, qz.at[n], qz_s.at[n], qz_r.at[n], dev)

        qsum[far] = qpart[c, far] + qcore[far]
        go(0, qsum.at[far, 0], up_dev)
        go(1, qsum.at[far, 1], dn_dev)
        qsum[nxt] = qpart[c, nxt] + qcore[nxt]
        go(2, qsum.at[nxt, 1], up_dev)
        qsum[prv] = qpart[c, prv] + qcore[prv]
        go(3, qsum.at[prv, 0], dn_dev)

    def query_pass_on():
        for n, (to, half, dev) in enumerate(((nxt, 0, up_dev), (prv, 1, dn_dev))):
            qcp[n].wait_recv()
            qfwd[n] = qsum[to, half] + qz[n]
            qcp[4 + n] = send(qfwd.at[n], qz.at[4 + n], qz_s.at[4 + n], qz_r.at[4 + n], dev)

    def spread_matrix(h):
        out = iota((128, 64), 0)
        return onehot(
            (((out >> 2) & 1) == h) & (iota((128, 64), 1) == (out >> 3) * 4 + (out & 3))
        )

    def turn(v, cosine, sine):
        width = v.shape[1]
        even = (iota(v.shape, 1) & 1) == 0
        swap = jnp.where(even, pltpu.roll(v, width - 1, 1), pltpu.roll(v, 1, 1))
        return v * cosine + swap * jnp.where(even, -sine, sine)

    acp = {}

    def query_finish():
        for n in (3, 2, 4, 5):
            qcp[n].wait_recv()
        full = jnp.concatenate(
            [
                qpart[c, z, 0] + qcore[z, 0] + (qz[4] + qz[3]),
                qpart[c, z, 1] + qcore[z, 1] + (qz[2] + qz[5]),
            ],
            axis=0,
        )
        cosine, sine = tab[0], tab[1]
        q0 = turn(full[:, 0:256], cosine, sine).astype(BF16)
        q1 = turn(full[:, 256:512], cosine, sine).astype(BF16)
        group = j // 4
        low, is_key = group == 0, group < 2
        pc = jnp.where(is_key, jnp.where(low, cosine[:, 0:128], cosine[:, 128:256]), 1.0)
        ps = jnp.where(is_key, jnp.where(low, sine[:, 0:128], sine[:, 128:256]), 0.0)
        pr = turn(full[:, QC:], pc, ps).astype(BF16)
        m0, m1 = spread_matrix(0), spread_matrix(1)
        ab[:, :, 0:256] = (dot(m0, q0) + dot(m1, q1)).reshape(16, 8, 256)
        ab[:, :, 256:384] = dot(m0, pr).reshape(16, 8, 128)
        for k in range(1, 16):
            to = (j + k) % 16
            acp[k] = send(ab.at[to], arecv.at[j], a_s.at[k], a_r.at[k], (i, to))
        arecv[j] = ab[j]

    bcp = {}

    def attention():
        for k in range(1, 16):
            acp[k].wait_recv()
        queries = arecv[:, :, 0:256].reshape(128, 256).astype(BF16)
        out = iota((128, 128), 0)
        inn = iota((128, 128), 1)
        order = onehot(
            ((out >> 5) == (inn & 3)) & (((out >> 1) & 15) == (inn >> 3)) & ((out & 1) == ((inn >> 2) & 1))
        )
        qall[...] = dot(order, queries).astype(BF16).reshape(OWN, 32, HEAD)
        for g in range(4):
            cols = arecv[4 * g, :, 256:384]
            for s in range(1, 4):
                cols = cols + arecv[4 * g + s, :, 256:384]
            npair[:, 128 * g : 128 * g + 128] = cols
        new_pair[...] = npair[0:OWN, :].astype(BF16)

        def body(k, carry):
            q = qall[k]
            s = lax.dot_general(
                q, ck[k], (((1,), (1,)), ((), ())), preferred_element_type=F32
            ) * (HEAD ** -0.5)
            pair = npair[pl.ds(k, 1), :]
            fresh = jnp.sum(q.astype(F32) * pair[:, 0:HEAD], axis=1, keepdims=True) * (HEAD ** -0.5)
            valid = iota((32, SLOTS), 1) < lengths[OWN * j + k]
            top = jnp.maximum(jnp.max(jnp.where(valid, s, -1e30), axis=1, keepdims=True), fresh)
            w = jnp.where(valid, jnp.exp(s - top), 0.0)
            fw = jnp.exp(fresh - top)
            tot = jnp.sum(w, axis=1, keepdims=True) + fw
            probs = (w / tot).astype(BF16)
            fp = (fw / tot).astype(BF16).astype(F32)
            attk[k] = (dot(probs, cv[k]) + fp * pair[:, HEAD:]).astype(BF16)
            return carry

        lax.fori_loop(0, OWN, body, 0)
        back = onehot(
            ((inn >> 5) == (out & 3)) & (((inn >> 1) & 15) == (out >> 3)) & ((inn & 1) == ((out >> 2) & 1))
        )
        bb[...] = dot(back, attk[...].reshape(128, HEAD)).reshape(16, 8, HEAD)
        for k in range(1, 16):
            to = (j + k) % 16
            bcp[k] = send(bb.at[to], brecv.at[j], b_s.at[k], b_r.at[k], (i, to))
        brecv[j] = bb[j]

    attz, attc = {}, {}

    def attended_spread():
        for k in range(1, 16):
            bcp[k].wait_recv()
        rows = brecv[...].reshape(128, HEAD).astype(BF16)
        inn = iota((64, 128), 1)
        for h in (0, 1):
            gather = onehot(
                (((inn >> 2) & 1) == h) & (iota((64, 128), 0) == (inn >> 3) * 4 + (inn & 3))
            )
            att[i, :, HEAD * h : HEAD * h + HEAD] = dot(gather, rows).astype(BF16)
        block = att.at[i]
        for n, k in enumerate((1, 3, 2)):
            attz[n] = send(block, block, attz_s.at[n], attz_r.at[n], zdev(k))
        attc[3] = send(block, block, attc_s.at[3], attc_r.at[3], sib)

    def attended_forward():
        for n, k in enumerate((1, 3, 2)):
            attz[n].wait_recv()
            block = att.at[((z + 4 - k) % 4) * 2 + c]
            attc[n] = send(block, block, attc_s.at[n], attc_r.at[n], sib)

    r1 = {}

    def along_x(d):
        return (i, y * 4 + (x + d) % 4)

    def along_y(d):
        return (i, ((y + d) % 4) * 4 + x)

    def wait_attended():
        for k in range(4):
            attc[k].wait_recv()

    def out_product(t):
        blocks = []
        for dy in range(4):
            xx = (x + (t - dy) % 4) % 4
            start = pl.multiple_of((xx % 2) * BLK, BLK)
            blocks.append(att[2 * ((y + dy) % 4) + xx // 2, pl.ds(start, BLK), :])
        rows = jnp.concatenate(blocks, axis=0)
        for n in range(2):
            cols = slice(512 * n, 512 * n + 512)
            v = total[t, :, cols] + dot(rows, out_w[:, cols])
            dpart[t, :, :, cols] = v.astype(BF16).reshape(4, BLK, 512)
        for dy in range(4):
            dx = (t - dy) % 4
            if dx:
                r1[0, dx, dy] = send(
                    dpart.at[t, dy, top], r1x.at[dx, dy], r1x_s.at[dx, dy], r1x_r.at[dx, dy], along_x(dx)
                )
            if dy:
                r1[1, dy, dx] = send(
                    dpart.at[t, dy, low], r1y.at[dy, dx], r1y_s.at[dy, dx], r1y_r.at[dy, dx], along_y(dy)
                )

    def gathered(axis, d):
        rows, recv = (top, r1x) if axis == 0 else (low, r1y)
        v = dpart[d, d if axis == 0 else 0, rows].astype(F32)
        for e in (1, 2, 3):
            r1[axis, e, d].wait_recv()
            v = v + recv[e, d].astype(F32)
        return v

    loads["gate"].wait()
    loads["up"].wait()
    wait_tokens(0)
    gate_up(0, "give")
    gate_up(0, "keep")
    core_add(0)
    loads["query"].wait()
    query_product(0)
    wait_tokens(1)
    query_product(1)
    wait_tokens(2)
    query_product(2)
    wait_tokens(3)
    query_product(3)
    query_send()
    pass_on(0)
    gate_up(1, "give")
    query_core_add()
    gate_up(1, "keep")
    gate_up(2, "give")
    query_pass_on()
    core_add(1)
    finish_hidden(0)
    gate_up(2, "keep")
    core_add(2)
    gate_up(3, "give")
    query_finish()
    pass_on(1)
    gate_up(3, "keep")
    core_add(3)
    forward_hidden(0)
    pass_on(2)
    loads["ck"].wait()
    loads["cv"].wait()
    attention()
    finish_hidden(1)
    pass_on(3)
    forward_far(0)
    forward_hidden(1)
    finish_hidden(2)
    loads["down"].wait()
    down(0)
    attended_spread()
    finish_hidden(3)
    forward_far(1)
    forward_hidden(2)
    down(1)
    attended_forward()
    forward_hidden(3)
    loads["out"].wait()
    wait_attended()
    out_product(0)
    out_product(1)
    forward_far(2)
    down(2)
    out_product(2)
    forward_far(3)
    down(3)
    out_product(3)

    r2 = {}
    for d in (2, 1, 3):
        mid[0, d] = gathered(0, d).astype(BF16)
        r2[0, d] = send(mid.at[0, d], r2x.at[d], r2x_s.at[d], r2x_r.at[d], along_y(d))
        mid[1, d] = gathered(1, d).astype(BF16)
        r2[1, d] = send(mid.at[1, d], r2y.at[d], r2y_s.at[d], r2y_r.at[d], along_x(d))
    for axis, (rows, recv) in enumerate(((top, r2x), (low, r2y))):
        result = tokens[rows, :].astype(F32) + gathered(axis, 0)
        for d in (1, 3, 2):
            r2[axis, d].wait_recv()
            result = result + recv[d].astype(F32)
        mixed[rows, :] = result.astype(BF16)
    for cp in pending:
        cp.wait_send()


def local(
    tokens, gain, gate_weight, up_weight, down_weight, query_weight, pair_weight, out_weight,
    cache_k, cache_v, lengths,
):
    freq = np.power(10000.0, -2.0 * (np.arange(HEAD) // 2) / HEAD).astype(np.float32)[None, :]
    vm = pl.BlockSpec(memory_space=pltpu.VMEM)
    sm = pl.BlockSpec(memory_space=pltpu.SMEM)
    hb = pl.BlockSpec(memory_space=pl.ANY)
    dma = pltpu.SemaphoreType.DMA
    v = pltpu.VMEM
    return pl.pallas_call(
        kernel,
        out_shape=(
            jax.ShapeDtypeStruct((BLK, DEPTH), BF16),
            jax.ShapeDtypeStruct((OWN, 2 * HEAD), BF16),
        ),
        in_specs=[hb, hb, sm, hb, hb, hb, hb, hb, hb, hb, hb, hb],
        out_specs=(vm, vm),
        scratch_shapes=[
            v((BLK, DEPTH), BF16), v((1, DEPTH), F32), v((1, HEAD), F32), v((PAIR, DEPTH), BF16),
            v((DEPTH, HID), BF16), v((DEPTH, HID), BF16), v((HID, DEPTH), BF16),
            v((DEPTH, QC), BF16), v((QC, DEPTH), BF16),
            v((OWN, SLOTS, HEAD), BF16), v((OWN, SLOTS, HEAD), BF16), v((DEPTH, 128), BF16),
            v((8, 8, 128), F32), v((16, 8, 128), F32), v((16, BLK, DEPTH), BF16),
            v((16, BLK, DEPTH), BF16),
            v((T, 2, 4, PIECE, 512), BF16), v((T, 4, PIECE, 512), BF16),
            v((T, 4, PIECE, 512), BF16), v((T, 2, 64, 512), BF16), v((T, 6, 64, 512), BF16),
            v((T, PIECE, HID), BF16),
            v((2, 4, 2, BLK, QC + 128), F32), v((4, 2, BLK, QC + 128), F32),
            v((4, 2, BLK, QC + 128), F32), v((2, BLK, QC + 128), F32), v((6, BLK, QC + 128), F32),
            v((2, 64, HEAD), F32), v((16, 8, 384), F32), v((16, 8, 384), F32),
            v((OWN, 32, HEAD), BF16), v((8, 2 * HEAD), F32), v((OWN, 32, HEAD), BF16),
            v((16, 8, HEAD), F32), v((16, 8, HEAD), F32), v((8, 64, QC), BF16),
            v((T, PIECE, DEPTH), F32), v((T, 4, BLK, DEPTH), BF16), v((4, 4, 16, DEPTH), BF16),
            v((4, 4, 16, DEPTH), BF16), v((4, 16, DEPTH), BF16), v((4, 16, DEPTH), BF16),
            v((2, 4, 16, DEPTH), BF16),
            dma((11,)), dma((8,)), dma((8,)), dma((16,)), dma((16,)), dma((16,)), dma((16,)),
            dma((16, 2)), dma((16, 2)), dma((T,)), dma((T,)),
            dma((T, 6)), dma((T, 6)), dma((T, 4)), dma((T, 4)), dma((T, 4)), dma((T, 4)),
            dma((1,)), dma((1,)), dma((6,)), dma((6,)), dma((16,)), dma((16,)),
            dma((16,)), dma((16,)), dma((4,)), dma((4,)), dma((4,)), dma((4,)),
            dma((4, 4)), dma((4, 4)), dma((4, 4)), dma((4, 4)), dma((4,)), dma((4,)), dma((4,)), dma((4,)),
        ],
        compiler_params=pltpu.CompilerParams(
            collective_id=0, has_side_effects=True, vmem_limit_bytes=56 * 1024 * 1024
        ),
        cost_estimate=pl.CostEstimate(
            flops=2 * ROWS * DEPTH * 7200, bytes_accessed=20 * 1024 * 1024, transcendentals=1 << 20
        ),
        name="layer",
    )(
        tokens, gain.reshape(1, DEPTH), lengths, jnp.asarray(freq), gate_weight, up_weight,
        down_weight, query_weight, pair_weight.T, out_weight, cache_k, cache_v,
    )


def solution(mesh):
    in_specs = (
        P("gy", "gx"),
        P("gx"),
        P("gx", "gy"),
        P("gx", "gy"),
        P("gy", "gx"),
        P("gx", "gy"),
        P("gx", "gy"),
        P("gy", "gx"),
        P(("gx", "gy"), None, None),
        P(("gx", "gy"), None, None),
        P("gx"),
    )
    out_specs = (P("gy", "gx"), P(("gx", "gy"), None))
    return jax.shard_map(local, mesh=mesh, in_specs=in_specs, out_specs=out_specs, check_vma=False)
```
